32 devices in a mesh: section: 2 (over y), expert: 8 (over z, x), dp: 2 (over core).
Axes of the slice: x: 2, y: 2, z: 4, core: 2. Of those that a mesh axis runs over, the one named last changes fastest.
Arguments:
- tokens: bfloat16 [256, 3072], P(('expert', 'dp')), may hold values from -6 to 6
- grad_out: bfloat16 [256, 3072], P(('expert', 'dp')), may hold values from -6 to 6
- expert_ids: int32 [256, 2], P(('expert', 'dp')), may hold values from 0 to 3, as said below
- gate_probs: float32 [256, 2], P(('expert', 'dp')), may hold values from 0.1 to 0.9
- gate_weight: bfloat16 [3072, 32768], P('dp', ('expert', 'section')), may hold values from -0.109375 to 0.109375
- up_weight: bfloat16 [3072, 32768], P('dp', ('expert', 'section')), may hold values from -0.109375 to 0.109375
- down_weight: bfloat16 [3072, 32768], P('dp', ('expert', 'section')), may hold values from -0.0625 to 0.0625
Outputs:
- moe_out: bfloat16 [256, 3072], P(('expert', 'dp'), 'section')
- grad_tokens: bfloat16 [256, 3072], P(('expert', 'dp'), 'section')
- grad_gate: bfloat16 [3072, 32768], P('dp', ('expert', 'section'))
- grad_up: bfloat16 [3072, 32768], P('dp', ('expert', 'section'))
- grad_down: bfloat16 [3072, 32768], P('dp', ('expert', 'section'))
The draws below stay inside these ranges and needn't reach their ends.
Inputs may be any that keep to these rules, and one draw needn't show every extreme that they name: `expert_ids`: each token names two different experts. Among the 16 tokens of one index of expert and dp (aligned blocks of 16 rows) no expert is named more than 12 times. For each index of dp one expert, drawn from the seed, is named exactly 12 times in every block of that index; block b has dp index b % 2.
All inputs are finite; a program needn't handle non-finite values.
Results may differ from the reference program's by a relative error of at most 0.015.
Values may be sent and summed in bfloat16 or wider, within the bound.
No kernel may reach another device: no remote copies, remote signals or barrier semaphores. Data moves between devices by JAX's collectives and lax.ppermute only.
A program may use at most 256 MiB of HBM per device.

```python
import jax
import jax.numpy as jnp
from jax import lax

D = 3072
EXP = 4
FF = 8192
TD = 16
CAP = 12
TOKENS = 256
N_DP = 2


def draw_expert_ids(key, part):
    blocks = TOKENS // TD
    key_hot, key_offset, key_rank, key_flip = jax.random.split(key, 4)
    hot_expert = jax.random.randint(key_hot, (N_DP,), 0, EXP)
    offsets = jax.random.randint(key_offset, (blocks,), 0, EXP - 1)
    rank_keys = jax.random.split(key_rank, blocks)
    ranks = jax.vmap(lambda one_key: jax.random.permutation(one_key, TD))(rank_keys)
    flips = jax.random.randint(key_flip, (blocks, TD), 0, 2)
    block_hot = hot_expert[jnp.arange(blocks) % N_DP][:, None]
    cycle = (ranks + offsets[:, None]) % (EXP - 1)
    is_hot = ranks < CAP
    first_pick = jnp.where(is_hot, block_hot, (block_hot + 1 + (cycle + 1) % (EXP - 1)) % EXP)
    second_pick = jnp.where(is_hot, (block_hot + 1 + cycle) % EXP, (block_hot + 1 + (cycle + 2) % (EXP - 1)) % EXP)
    column_a = jnp.where(flips == 1, second_pick, first_pick)
    column_b = jnp.where(flips == 1, first_pick, second_pick)
    return jnp.stack([column_a, column_b], axis=-1).reshape(TOKENS, 2).astype(jnp.int32)


def block_scale(own_key, dims, shards, low, top_value):
    def one(axis_at, blocks):
        draws = jax.random.uniform(jax.random.fold_in(jax.random.fold_in(own_key, 6), axis_at), (blocks,), jnp.float32, low / len(shards), top_value / len(shards))
        return jnp.repeat(jnp.exp(draws), dims[axis_at] // blocks).reshape((-1,) + (1,) * (len(dims) - axis_at - 1))

    factor_of = one(*shards[0])
    for cut in shards[1:]:
        factor_of = factor_of * one(*cut)
    return factor_of


def centred(key, extent, spread, limit, pieces=(), held_as=jnp.bfloat16):
    loudness = block_scale(key, extent, pieces, -0.22, 0.18) if pieces else 1.0
    drawn = jax.random.normal(key, extent, jnp.float32) * spread * loudness
    return jnp.minimum(jnp.maximum(drawn, -limit), limit).astype(held_as)


def setup_inputs(seed: int = 0) -> dict:
    key_of = jax.random.split(jax.random.key(seed), 8)
    return {
        "tokens": centred(key_of[0], (TOKENS, D), 1.0, 6.0, ((0, 16),)),
        "grad_out": centred(key_of[1], (TOKENS, D), 1.0, 6.0, ((0, 16),)),
        "expert_ids": draw_expert_ids(jax.random.fold_in(key_of[7], 71), 0),
        "gate_probs": jnp.clip(0.1 + 0.79999997 * jax.random.uniform(key_of[3], (TOKENS, 2), jnp.float32) ** block_scale(key_of[3], (TOKENS, 2), ((0, 16),), -0.2, 0.2), 0.1, 0.9),
        "gate_weight": centred(key_of[4], (D, EXP * FF), D ** -0.5, 0.109375, ((0, 2), (1, 16))),
        "up_weight": centred(key_of[5], (D, EXP * FF), D ** -0.5, 0.109375, ((0, 2), (1, 16))),
        "down_weight": centred(key_of[6], (D, EXP * FF), FF ** -0.5, 0.0625, ((0, 2), (1, 16))),
    }


def half_sums(left, right):
    blocks = TOKENS // (TD * N_DP)
    left_halves = left.reshape(blocks, N_DP, TD, left.shape[1])
    right_halves = right.reshape(blocks, N_DP, TD, right.shape[1])
    summed = jnp.zeros((left.shape[1], right.shape[1]), jnp.float32)
    for half_index in range(N_DP):
        left_part = left_halves[:, half_index].reshape(-1, left.shape[1])
        right_part = right_halves[:, half_index].reshape(-1, right.shape[1])
        partial_value = jnp.dot(left_part.T, right_part, preferred_element_type=jnp.float32).astype(jnp.bfloat16)
        partial_value = lax.optimization_barrier(partial_value)
        summed = summed + partial_value.astype(jnp.float32)
    return summed.astype(jnp.bfloat16)


def reference(tokens, grad_out, expert_ids, gate_probs, gate_weight, up_weight, down_weight):
    moe_sum = jnp.zeros((TOKENS, D), jnp.float32)
    input_sum = jnp.zeros((TOKENS, D), jnp.float32)
    grads_gate = []
    grads_up = []
    grads_down = []
    for expert in range(EXP):
        gate_share = jnp.sum(jnp.where(expert_ids == expert, gate_probs, 0.0), axis=1)
        w_gate = gate_weight[:, expert * FF:(expert + 1) * FF]
        w_up = up_weight[:, expert * FF:(expert + 1) * FF]
        w_down = down_weight[:, expert * FF:(expert + 1) * FF]
        gate_pre = jnp.dot(tokens, w_gate, preferred_element_type=jnp.float32)
        up_pre = jnp.dot(tokens, w_up, preferred_element_type=jnp.float32)
        sigmoid_gate = jax.nn.sigmoid(gate_pre)
        silu_value = gate_pre * sigmoid_gate
        activation = (silu_value * up_pre).astype(jnp.bfloat16)
        expert_out = jnp.dot(activation, w_down.T, preferred_element_type=jnp.float32)
        moe_sum = moe_sum + gate_share[:, None] * expert_out
        scaled_grad = (gate_share[:, None] * grad_out.astype(jnp.float32)).astype(jnp.bfloat16)
        act_grad = jnp.dot(scaled_grad, w_down, preferred_element_type=jnp.float32)
        up_grad = (act_grad * silu_value).astype(jnp.bfloat16)
        gate_grad = (act_grad * up_pre * sigmoid_gate * (1.0 + gate_pre * (1.0 - sigmoid_gate))).astype(jnp.bfloat16)
        input_sum = input_sum + jnp.dot(gate_grad, w_gate.T, preferred_element_type=jnp.float32)
        input_sum = input_sum + jnp.dot(up_grad, w_up.T, preferred_element_type=jnp.float32)
        grads_gate.append(half_sums(tokens, gate_grad))
        grads_up.append(half_sums(tokens, up_grad))
        grads_down.append(half_sums(scaled_grad, activation))
    return (moe_sum.astype(jnp.bfloat16), input_sum.astype(jnp.bfloat16),
            jnp.concatenate(grads_gate, axis=1), jnp.concatenate(grads_up, axis=1),
            jnp.concatenate(grads_down, axis=1))
```

```python
import jax
import jax.numpy as jnp
from jax import lax
from jax.sharding import PartitionSpec as P

EXP = 4
CAP = 12
BF = jnp.bfloat16
F32 = jnp.float32


def contract_rows(left, right):
    return lax.dot_general(left, right, (((0,), (0,)), ((), ())), preferred_element_type=F32)


def contract_cols(left, right):
    return lax.dot_general(left, right, (((1,), (1,)), ((), ())), preferred_element_type=F32)


def slot_tables(id_match, capacity):
    chosen = jnp.any(id_match, axis=2)
    slot_rank = jnp.cumsum(chosen.astype(jnp.int32), axis=1) - 1
    slot_index = jnp.arange(capacity, dtype=jnp.int32)
    return jnp.logical_and(
        chosen[:, None, :], slot_rank[:, None, :] == slot_index[None, :, None]
    )


def general(tokens, grad_out, expert_ids, gate_probs, gate_weight, up_weight, down_weight):
    expert_devices = lax.axis_size("expert")
    model_width = tokens.shape[1]
    group_size = expert_devices // EXP
    gate_full, up_full, down_full = (
        lax.all_gather(weight, "dp", axis=0, tiled=True)
        for weight in (gate_weight, up_weight, down_weight)
    )
    own_match = expert_ids[None, :, :] == jnp.arange(EXP, dtype=jnp.int32)[:, None, None]
    own_picks = slot_tables(own_match, CAP).astype(F32)
    own_share = jnp.sum(jnp.where(own_match, gate_probs[None, :, :], 0.0), axis=2)
    own_scaled = (own_share[:, :, None] * grad_out[None].astype(F32)).astype(BF)
    pick_bf = own_picks.astype(BF)
    send_tokens = jnp.einsum("ect,td->ecd", pick_bf, tokens, preferred_element_type=F32).astype(BF)
    send_grads = jnp.einsum("ect,etd->ecd", pick_bf, own_scaled, preferred_element_type=F32).astype(BF)

    def swap(rows):
        return lax.all_to_all(rows, "expert", split_axis=0, concat_axis=0, tiled=True)

    slot_tokens = swap(jnp.repeat(send_tokens, group_size, axis=0)).reshape(-1, model_width)
    slot_grads = swap(jnp.repeat(send_grads, group_size, axis=0)).reshape(-1, model_width)
    gate_pre = jnp.dot(slot_tokens, gate_full, preferred_element_type=F32)
    up_pre = jnp.dot(slot_tokens, up_full, preferred_element_type=F32)
    act_grad = jnp.dot(slot_grads, down_full, preferred_element_type=F32)
    activation, up_grad, gate_grad = pointwise(gate_pre, up_pre, act_grad)
    partial_out = contract_cols(activation, down_full)
    partial_in = contract_cols(gate_grad, gate_full) + contract_cols(up_grad, up_full)
    summed_grads = lax.psum_scatter(
        jnp.concatenate(
            [
                contract_rows(slot_tokens, gate_grad),
                contract_rows(slot_tokens, up_grad),
                contract_rows(slot_grads, activation),
            ],
            axis=1,
        ).astype(BF),
        "dp",
        scatter_dimension=0,
        tiled=True,
    )
    hidden = gate_weight.shape[1]
    weighted_picks = own_picks * own_share[:, None, :]
    back_out = swap(partial_out.reshape(expert_devices, CAP, model_width).astype(BF)).astype(F32)
    back_in = swap(partial_in.reshape(expert_devices, CAP, model_width).astype(BF)).astype(F32)
    sum_out = back_out.reshape(EXP, group_size, CAP, model_width).sum(axis=1)
    sum_in = back_in.reshape(EXP, group_size, CAP, model_width).sum(axis=1)
    token_out = jnp.einsum("ect,ecd->td", weighted_picks, sum_out, precision=lax.Precision.HIGHEST)
    token_in = jnp.einsum("ect,ecd->td", own_picks, sum_in, precision=lax.Precision.HIGHEST)
    return (
        lax.psum_scatter(token_out.astype(BF), "section", scatter_dimension=1, tiled=True),
        lax.psum_scatter(token_in.astype(BF), "section", scatter_dimension=1, tiled=True),
        summed_grads[:, :hidden],
        summed_grads[:, hidden : 2 * hidden],
        summed_grads[:, 2 * hidden :],
    )


def pointwise(gate_pre, up_pre, act_grad):
    sigmoid_gate = jax.nn.sigmoid(gate_pre)
    silu_value = gate_pre * sigmoid_gate
    activation = (silu_value * up_pre).astype(BF)
    up_grad = (act_grad * silu_value).astype(BF)
    gate_grad = (act_grad * up_pre * sigmoid_gate * (1.0 + gate_pre * (1.0 - sigmoid_gate))).astype(BF)
    return activation, up_grad, gate_grad


def swap_expert(rows):
    size = lax.axis_size("expert")
    return lax.ppermute(rows, "expert", [(i, i ^ 1) for i in range(size)])


def swap_section(rows):
    return lax.ppermute(rows, "section", [(0, 1), (1, 0)])


def swap_dp(rows):
    return lax.ppermute(rows, "dp", [(0, 1), (1, 0)])


def turn(rows, shift):
    size = lax.axis_size("expert")
    pairs = []
    for s in range(2):
        for i in range(size):
            for d in range(2):
                j = (i + 2 * shift) % size
                pairs.append(((s * size + i) * 2 + d, (d * size + j) * 2 + s))
    return lax.ppermute(rows, ("section", "expert", "dp"), pairs)


def paired(tokens, grad_out, expert_ids, gate_probs, gate_weight, up_weight, down_weight):
    half = gate_weight.shape[0]
    count = tokens.shape[0]
    section = lax.axis_index("section")
    plane = lax.axis_index("expert") // 2
    experts = (plane + jnp.arange(EXP, dtype=jnp.int32)) % EXP
    match = expert_ids[None, :, :] == experts[:, None, None]
    picks = slot_tables(match, CAP)
    share = jnp.sum(jnp.where(match, gate_probs[None, :, :], 0.0), axis=2)
    slot_gate = jnp.sum(jnp.where(picks, share[:, None, :], 0.0), axis=2)
    none = jnp.zeros_like(picks)
    pick_both = jnp.concatenate(
        [jnp.concatenate([picks, none], axis=2), jnp.concatenate([none, picks], axis=2)], axis=1
    ).reshape(EXP * 2 * CAP, 2 * count).astype(BF)
    scale = jnp.concatenate([jnp.ones_like(slot_gate), slot_gate], axis=1).reshape(-1, 1)
    rows = jnp.concatenate([tokens, grad_out], axis=0)
    rows = lax.dynamic_slice_in_dim(rows, section * half, half, axis=1)
    payload = (jnp.dot(pick_both, rows, preferred_element_type=F32) * scale).astype(BF)
    got = [turn(payload[k * 2 * CAP : (k + 1) * 2 * CAP], k) for k in range(EXP)]
    own_t = jnp.concatenate([g[:CAP] for g in got], axis=0)
    own_g = jnp.concatenate([g[CAP:] for g in got], axis=0)
    n = EXP * CAP
    xt = swap_expert(own_t)
    yg = swap_section(own_g)
    yt = swap_section(jnp.concatenate([own_t, xt], axis=0))
    two_g = jnp.concatenate([own_g, yg], axis=0)
    xg = swap_expert(two_g)
    slot_t = jnp.concatenate([own_t, yt[:n], xt, yt[n:]], axis=0)
    slot_g = jnp.concatenate([two_g, xg], axis=0)

    gate_p = jnp.dot(slot_t, gate_weight, preferred_element_type=F32)
    up_p = jnp.dot(slot_t, up_weight, preferred_element_type=F32)
    act_p = jnp.dot(slot_g, down_weight, preferred_element_type=F32)
    gate_pre = gate_p + swap_dp(gate_p.astype(BF)).astype(F32)
    up_pre = up_p + swap_dp(up_p.astype(BF)).astype(F32)
    act_grad = act_p + swap_dp(act_p.astype(BF)).astype(F32)
    activation, up_grad, gate_grad = pointwise(gate_pre, up_pre, act_grad)

    part_out = contract_cols(activation, down_weight).astype(BF)
    part_in = (contract_cols(gate_grad, gate_weight) + contract_cols(up_grad, up_weight)).astype(BF)
    grad_gate = contract_rows(slot_t, gate_grad).astype(BF)
    grad_up = contract_rows(slot_t, up_grad).astype(BF)
    grad_down = contract_rows(slot_g, activation).astype(BF)

    def add(a, b):
        return (a.astype(F32) + b.astype(F32)).astype(BF)

    two_out = add(part_out[: 2 * n], swap_expert(part_out[2 * n :]))
    one_out = add(two_out[:n], swap_section(two_out[n:]))
    two_in = add(
        jnp.concatenate([part_in[:n], part_in[2 * n : 3 * n]], axis=0),
        swap_section(jnp.concatenate([part_in[n : 2 * n], part_in[3 * n :]], axis=0)),
    )
    one_in = add(two_in[:n], swap_expert(two_in[n:]))
    back = [
        turn(
            jnp.concatenate(
                [one_out[k * CAP : (k + 1) * CAP], one_in[k * CAP : (k + 1) * CAP]], axis=0
            ),
            -k,
        )
        for k in range(EXP)
    ]
    back = jnp.concatenate(back, axis=0)
    per_choice = [
        jnp.logical_and(picks, match[:, None, :, j]) for j in range(2)
    ]
    blank = jnp.zeros_like(picks)
    spread = jnp.concatenate(
        [
            jnp.concatenate([per_choice[0], per_choice[1], blank], axis=2),
            jnp.concatenate([blank, blank, picks], axis=2),
        ],
        axis=1,
    ).reshape(EXP * 2 * CAP, 3 * count).astype(BF)
    found = contract_rows(spread, back)
    moe_out = (
        gate_probs[:, 0:1] * found[:count] + gate_probs[:, 1:2] * found[count : 2 * count]
    ).astype(BF)
    grad_tokens = found[2 * count :].astype(BF)
    return moe_out, grad_tokens, grad_gate, grad_up, grad_down


def solution(mesh):
    sizes = mesh.shape
    pairs = sizes["section"] == 2 and sizes["dp"] == 2 and sizes["expert"] == 2 * EXP
    return jax.shard_map(
        paired if pairs else general,
        mesh=mesh,
        in_specs=(
            P(("expert", "dp"), None),
            P(("expert", "dp"), None),
            P(("expert", "dp"), None),
            P(("expert", "dp"), None),
            P("dp", ("expert", "section")),
            P("dp", ("expert", "section")),
            P("dp", ("expert", "section")),
        ),
        out_specs=(
            P(("expert", "dp"), "section"),
            P(("expert", "dp"), "section"),
            P("dp", ("expert", "section")),
            P("dp", ("expert", "section")),
            P("dp", ("expert", "section")),
        ),
        check_vma=False,
    )
```

```python
import math

import jax
import jax.numpy as jnp
from jax import lax
from jax.experimental import pallas as pl
from jax.experimental.pallas import tpu as pltpu
from jax.sharding import PartitionSpec as P

EXP = 4
CAP = 12
BF = jnp.bfloat16
F32 = jnp.float32
TILE = 512


def contract_rows(left, right):
    return lax.dot_general(left, right, (((0,), (0,)), ((), ())), preferred_element_type=F32)


def contract_cols(left, right):
    return lax.dot_general(left, right, (((1,), (1,)), ((), ())), preferred_element_type=F32)


def slot_tables(id_match, capacity):
    chosen = jnp.any(id_match, axis=2)
    slot_rank = jnp.cumsum(chosen.astype(jnp.int32), axis=1) - 1
    slot_index = jnp.arange(capacity, dtype=jnp.int32)
    return jnp.logical_and(
        chosen[:, None, :], slot_rank[:, None, :] == slot_index[None, :, None]
    )


def general(tokens, grad_out, expert_ids, gate_probs, gate_weight, up_weight, down_weight):
    expert_devices = lax.axis_size("expert")
    model_width = tokens.shape[1]
    group_size = expert_devices // EXP
    gate_full, up_full, down_full = (
        lax.all_gather(weight, "dp", axis=0, tiled=True)
        for weight in (gate_weight, up_weight, down_weight)
    )
    own_match = expert_ids[None, :, :] == jnp.arange(EXP, dtype=jnp.int32)[:, None, None]
    own_picks = slot_tables(own_match, CAP).astype(F32)
    own_share = jnp.sum(jnp.where(own_match, gate_probs[None, :, :], 0.0), axis=2)
    own_scaled = (own_share[:, :, None] * grad_out[None].astype(F32)).astype(BF)
    pick_bf = own_picks.astype(BF)
    send_tokens = jnp.einsum("ect,td->ecd", pick_bf, tokens, preferred_element_type=F32).astype(BF)
    send_grads = jnp.einsum("ect,etd->ecd", pick_bf, own_scaled, preferred_element_type=F32).astype(BF)

    def swap(rows):
        return lax.all_to_all(rows, "expert", split_axis=0, concat_axis=0, tiled=True)

    slot_tokens = swap(jnp.repeat(send_tokens, group_size, axis=0)).reshape(-1, model_width)
    slot_grads = swap(jnp.repeat(send_grads, group_size, axis=0)).reshape(-1, model_width)
    gate_pre = jnp.dot(slot_tokens, gate_full, preferred_element_type=F32)
    up_pre = jnp.dot(slot_tokens, up_full, preferred_element_type=F32)
    act_grad = jnp.dot(slot_grads, down_full, preferred_element_type=F32)
    activation, up_grad, gate_grad = pointwise(gate_pre, up_pre, act_grad)
    partial_out = contract_cols(activation, down_full)
    partial_in = contract_cols(gate_grad, gate_full) + contract_cols(up_grad, up_full)
    summed_grads = lax.psum_scatter(
        jnp.concatenate(
            [
                contract_rows(slot_tokens, gate_grad),
                contract_rows(slot_tokens, up_grad),
                contract_rows(slot_grads, activation),
            ],
            axis=1,
        ).astype(BF),
        "dp",
        scatter_dimension=0,
        tiled=True,
    )
    hidden = gate_weight.shape[1]
    weighted_picks = own_picks * own_share[:, None, :]
    back_out = swap(partial_out.reshape(expert_devices, CAP, model_width).astype(BF)).astype(F32)
    back_in = swap(partial_in.reshape(expert_devices, CAP, model_width).astype(BF)).astype(F32)
    sum_out = back_out.reshape(EXP, group_size, CAP, model_width).sum(axis=1)
    sum_in = back_in.reshape(EXP, group_size, CAP, model_width).sum(axis=1)
    token_out = jnp.einsum("ect,ecd->td", weighted_picks, sum_out, precision=lax.Precision.HIGHEST)
    token_in = jnp.einsum("ect,ecd->td", own_picks, sum_in, precision=lax.Precision.HIGHEST)
    return (
        lax.psum_scatter(token_out.astype(BF), "section", scatter_dimension=1, tiled=True),
        lax.psum_scatter(token_in.astype(BF), "section", scatter_dimension=1, tiled=True),
        summed_grads[:, :hidden],
        summed_grads[:, hidden : 2 * hidden],
        summed_grads[:, 2 * hidden :],
    )


def pointwise(gate_pre, up_pre, act_grad):
    sigmoid_gate = jax.nn.sigmoid(gate_pre)
    silu_value = gate_pre * sigmoid_gate
    activation = (silu_value * up_pre).astype(BF)
    up_grad = (act_grad * silu_value).astype(BF)
    gate_grad = (act_grad * up_pre * sigmoid_gate * (1.0 + gate_pre * (1.0 - sigmoid_gate))).astype(BF)
    return activation, up_grad, gate_grad


def swap_expert(rows):
    size = lax.axis_size("expert")
    return lax.ppermute(rows, "expert", [(i, i ^ 1) for i in range(size)])


def swap_section(rows):
    return lax.ppermute(rows, "section", [(0, 1), (1, 0)])


def swap_plane(pieces):
    size = lax.axis_size("expert")
    both = [(s * size + i, (1 - s) * size + (i ^ 1)) for s in range(2) for i in range(size)]
    return [
        swap_section(pieces[0]),
        swap_expert(pieces[1]),
        lax.ppermute(pieces[2], ("section", "expert"), both),
    ]


ANYWHERE = pl.BlockSpec(memory_space=pl.ANY)
INSIDE = pl.BlockSpec(memory_space=pltpu.VMEM)


def params(mib):
    return pltpu.CompilerParams(vmem_limit_bytes=mib << 20)


def cost(flops, *arrays):
    moved = sum(a.size * a.dtype.itemsize for a in arrays)
    return pl.CostEstimate(flops=flops, bytes_accessed=moved, transcendentals=0)


def in_hbm(array):
    return pltpu.with_memory_space_constraint(array, pltpu.HBM)


def in_vmem(array):
    return pltpu.with_memory_space_constraint(array, pltpu.VMEM)


def pin_kernel(*refs):
    count = len(refs) // 2 - 1
    copies = [
        pltpu.make_async_copy(refs[i], refs[count + 1 + i], refs[-1].at[i]) for i in range(count)
    ]
    for copy in copies:
        copy.start()
    for copy in copies:
        copy.wait()


def pin(weights, after):
    count = len(weights)
    return pl.pallas_call(
        pin_kernel,
        out_shape=[pltpu.VMEM(weight.shape, weight.dtype) for weight in weights],
        in_specs=[ANYWHERE] * (count + 1),
        out_specs=[ANYWHERE] * count,
        scratch_shapes=[pltpu.SemaphoreType.DMA((count,))],
        cost_estimate=cost(0, *weights),
        compiler_params=params(1),
    )(*(in_hbm(weight) for weight in weights), after)


def gather_kernel(*refs):
    pieces, (w_ref, x_ref, out_ref) = refs[:-3], refs[-3:]
    rows = pieces[0].shape[0]
    for i, piece in enumerate(pieces):
        x_ref[i * rows : (i + 1) * rows] = piece[...]
    out_ref[...] = jnp.dot(x_ref[...], w_ref[...], preferred_element_type=F32).astype(BF)


def gather_project(pieces, weight):
    rows, (depth, hidden) = sum(piece.shape[0] for piece in pieces), weight.shape
    outs = [jax.ShapeDtypeStruct((rows, depth), BF), jax.ShapeDtypeStruct((rows, hidden), BF)]
    return pl.pallas_call(
        gather_kernel,
        out_shape=outs,
        in_specs=[INSIDE] * (len(pieces) + 1),
        out_specs=[INSIDE] * 2,
        cost_estimate=cost(2 * rows * depth * hidden, *pieces, *outs),
        compiler_params=params(14),
    )(*pieces, in_vmem(weight))


def project_kernel(x_ref, w_ref, out_ref):
    out_ref[...] = jnp.dot(x_ref[...], w_ref[...], preferred_element_type=F32).astype(BF)


def project(x, weight):
    rows, (depth, hidden) = x.shape[0], weight.shape
    out = jax.ShapeDtypeStruct((rows, hidden), BF)
    return pl.pallas_call(
        project_kernel,
        out_shape=out,
        in_specs=[INSIDE] * 2,
        out_specs=INSIDE,
        cost_estimate=cost(2 * rows * depth * hidden, x, out),
        compiler_params=params(12),
    )(x, in_vmem(weight))


def iota(shape, dim):
    return lax.broadcasted_iota(jnp.int32, shape, dim)


def slot_rows(ids_ref, plane):
    count = ids_ref.shape[1]
    shape = (EXP * 2 * CAP, count)
    row = iota(shape, 0)
    place = row % (2 * CAP)
    expert = (plane + row // (2 * CAP)) % EXP
    match = [ids_ref[j : j + 1, :] == expert for j in range(2)]
    chosen = jnp.logical_or(*match)
    before = (iota((count, count), 0) < iota((count, count), 1)).astype(F32)
    rank = jnp.dot(chosen.astype(F32), before, preferred_element_type=F32)
    picks = jnp.logical_and(chosen, rank == (place % CAP).astype(F32))
    return match, picks, place


def pack_kernel(tok_ref, grad_ref, ids_ref, probs_ref, *out_refs):
    half = out_refs[0].shape[1]
    start = pl.multiple_of(lax.axis_index("section") * half, half)
    match, picks, place = slot_rows(ids_ref, lax.axis_index("expert") // 2)
    share = jnp.where(match[0], probs_ref[0:1, :], 0.0) + jnp.where(match[1], probs_ref[1:2, :], 0.0)
    scale = jnp.sum(jnp.where(picks, share, 0.0), axis=1, keepdims=True)
    picks = picks.astype(BF)
    tok = jnp.dot(picks, tok_ref[:, pl.ds(start, half)], preferred_element_type=F32)
    grad = jnp.dot(picks, grad_ref[:, pl.ds(start, half)], preferred_element_type=F32)
    payload = jnp.where(place[:, 0:1] < CAP, tok, grad * scale)
    for k, out_ref in enumerate(out_refs):
        out_ref[...] = payload[k * 2 * CAP : (k + 1) * 2 * CAP].astype(BF)


def pack(tokens, grad_out, expert_ids, gate_probs, half):
    outs = [jax.ShapeDtypeStruct((2 * CAP, half), BF)] * EXP
    return pl.pallas_call(
        pack_kernel,
        out_shape=outs,
        in_specs=[INSIDE] * 4,
        out_specs=[INSIDE] * EXP,
        cost_estimate=cost(0, tokens, grad_out, *outs),
        compiler_params=params(8),
    )(tokens, grad_out, expert_ids.T, gate_probs.T)


def sorting():
    n = EXP * CAP
    sorted_row, row = iota((2 * n, 2 * n), 0), iota((2 * n, 2 * n), 1)
    k, j = row // (2 * CAP), row % (2 * CAP)
    place = jnp.where(j < CAP, k * CAP + j, n + k * CAP + j - CAP)
    return (sorted_row == place).astype(BF)


def stack(refs, held_ref):
    rows = refs[0].shape[0]
    for i, ref in enumerate(refs):
        held_ref[i * rows : (i + 1) * rows] = ref[...].astype(F32)
    return held_ref[...].astype(BF)


def part_kernel(*refs):
    refs, (tok_ref, grad_ref, held_ref) = refs[:EXP], refs[EXP:]
    rows = jnp.dot(sorting(), stack(refs, held_ref), preferred_element_type=F32).astype(BF)
    n = EXP * CAP
    tok_ref[...] = rows[:n]
    grad_ref[...] = rows[n:]


def part(got):
    width = got[0].shape[1]
    outs = [jax.ShapeDtypeStruct((EXP * CAP, width), BF)] * 2
    return pl.pallas_call(
        part_kernel,
        out_shape=outs,
        in_specs=[INSIDE] * EXP,
        out_specs=[INSIDE] * 2,
        scratch_shapes=[pltpu.VMEM((2 * EXP * CAP, width), F32)],
        cost_estimate=cost(0, *got, *outs),
        compiler_params=params(8),
    )(*got)


def join_kernel(*refs):
    outs, ins, sent = refs[:4], refs[4:8], refs[8:]

    def total(pieces):
        return sum(p[...].astype(F32) for p in pieces).astype(BF)

    rows = jnp.concatenate([total(outs), total(ins)], axis=0)
    rows = lax.dot_general(
        sorting(), rows, (((0,), (0,)), ((), ())), preferred_element_type=F32
    )
    for k, ref in enumerate(sent):
        ref[...] = rows[k * 2 * CAP : (k + 1) * 2 * CAP].astype(BF)


def join(outs, ins):
    width = outs[0].shape[1]
    sent = [jax.ShapeDtypeStruct((2 * CAP, width), BF)] * EXP
    return pl.pallas_call(
        join_kernel,
        out_shape=sent,
        in_specs=[INSIDE] * 8,
        out_specs=[INSIDE] * EXP,
        cost_estimate=cost(0, *outs, *ins, *sent),
        compiler_params=params(10),
    )(*outs, *ins)


def unpack_kernel(*refs):
    refs, (ids_ref, probs_ref, out_ref, in_ref, held_ref) = refs[:EXP], refs[EXP:]
    match, picks, place = slot_rows(ids_ref, lax.axis_index("expert") // 2)
    rows = stack(refs, held_ref)
    count = ids_ref.shape[1]
    same = iota((count, count), 0) == iota((count, count), 1)
    probs = [
        jnp.sum(jnp.where(same, probs_ref[j : j + 1, :], 0.0), axis=1, keepdims=True)
        for j in range(2)
    ]

    def found(where):
        return contract_rows(jnp.logical_and(picks, where).astype(BF), rows)

    first = place < CAP
    out_ref[...] = (
        probs[0] * found(jnp.logical_and(first, match[0]))
        + probs[1] * found(jnp.logical_and(first, match[1]))
    ).astype(BF)
    in_ref[...] = found(jnp.logical_not(first)).astype(BF)


def unpack(back, expert_ids, gate_probs):
    width = back[0].shape[1]
    outs = [jax.ShapeDtypeStruct((expert_ids.shape[0], width), BF)] * 2
    return pl.pallas_call(
        unpack_kernel,
        out_shape=outs,
        in_specs=[INSIDE] * (EXP + 2),
        out_specs=[INSIDE] * 2,
        scratch_shapes=[pltpu.VMEM((2 * EXP * CAP, width), F32)],
        cost_estimate=cost(0, *back, *outs),
        compiler_params=params(8),
    )(*back, expert_ids.T, gate_probs.T)


def spread(rows, refs):
    count = refs[0].shape[0]
    for i, ref in enumerate(refs):
        ref[...] = rows[i * count : (i + 1) * count].astype(BF)


def forward_kernel(g0_ref, g1_ref, u0_ref, u1_ref, w_ref, act_ref, *out_refs):
    hidden = act_ref.shape[1]
    tile = math.gcd(hidden, TILE)
    for at in range(0, hidden, tile):
        cut = slice(at, at + tile)
        gate_pre = g0_ref[:, cut].astype(F32) + g1_ref[:, cut].astype(F32)
        up_pre = u0_ref[:, cut].astype(F32) + u1_ref[:, cut].astype(F32)
        act_ref[:, cut] = (gate_pre * jax.nn.sigmoid(gate_pre) * up_pre).astype(BF)
    spread(contract_cols(act_ref[...], w_ref[...]), out_refs)


def forward(gates, ups, weight):
    rows, (depth, hidden) = gates[0].shape[0], weight.shape
    outs = [jax.ShapeDtypeStruct((rows, hidden), BF)]
    outs += [jax.ShapeDtypeStruct((rows // 4, depth), BF)] * 4
    return pl.pallas_call(
        forward_kernel,
        out_shape=outs,
        in_specs=[INSIDE] * 5,
        out_specs=[INSIDE] * 5,
        cost_estimate=cost(2 * rows * depth * hidden, *gates, *ups, *outs),
        compiler_params=params(16),
    )(*gates, *ups, in_vmem(weight))


def backward_kernel(
    g0_ref, g1_ref, u0_ref, u1_ref, a0_ref, a1_ref, wg_ref, wu_ref, dg_ref, du_ref, *out_refs
):
    hidden = dg_ref.shape[1]
    tile = math.gcd(hidden, TILE)
    for at in range(0, hidden, tile):
        cut = slice(at, at + tile)
        gate_pre = g0_ref[:, cut].astype(F32) + g1_ref[:, cut].astype(F32)
        up_pre = u0_ref[:, cut].astype(F32) + u1_ref[:, cut].astype(F32)
        act_grad = a0_ref[:, cut].astype(F32) + a1_ref[:, cut].astype(F32)
        _, up_grad, gate_grad = pointwise(gate_pre, up_pre, act_grad)
        dg_ref[:, cut] = gate_grad
        du_ref[:, cut] = up_grad
    spread(
        contract_cols(dg_ref[...], wg_ref[...]) + contract_cols(du_ref[...], wu_ref[...]), out_refs
    )


def backward(gates, ups, acts, gate_weight, up_weight):
    rows, (depth, hidden) = gates[0].shape[0], gate_weight.shape
    outs = [
        jax.ShapeDtypeStruct((rows, hidden), BF),
        jax.ShapeDtypeStruct((rows, hidden), BF),
    ] + [jax.ShapeDtypeStruct((rows // 4, depth), BF)] * 4
    return pl.pallas_call(
        backward_kernel,
        out_shape=outs,
        in_specs=[INSIDE] * 8,
        out_specs=[INSIDE] * 6,
        cost_estimate=cost(4 * rows * depth * hidden, *gates, *ups, *acts, *outs),
        compiler_params=params(20),
    )(*gates, *ups, *acts, in_vmem(gate_weight), in_vmem(up_weight))


def outer_kernel(x_ref, y_ref, out_ref, turned_ref, held_ref, sem):
    depth = held_ref.shape[0]
    tile = math.gcd(depth, 256)
    turned_ref[...] = x_ref[...].T
    copies = []
    for i, at in enumerate(range(0, depth, tile)):
        cut = slice(at, at + tile)
        held_ref[cut] = jnp.dot(
            turned_ref[cut], y_ref[...], preferred_element_type=F32
        ).astype(BF)
        copies.append(pltpu.make_async_copy(held_ref.at[cut], out_ref.at[cut], sem.at[i]))
        copies[-1].start()
    for copy in copies:
        copy.wait()


def outer(x, y):
    (rows, depth), hidden = x.shape, y.shape[1]
    out = jax.ShapeDtypeStruct((depth, hidden), BF)
    return pl.pallas_call(
        outer_kernel,
        out_shape=out,
        in_specs=[INSIDE] * 2,
        out_specs=ANYWHERE,
        scratch_shapes=[
            pltpu.VMEM((depth, rows), BF),
            pltpu.VMEM((depth, hidden), BF),
            pltpu.SemaphoreType.DMA((depth // math.gcd(depth, 256),)),
        ],
        cost_estimate=cost(2 * rows * depth * hidden, x, y, out),
        compiler_params=params(24),
    )(x, y)


def swap_dp(rows):
    return lax.ppermute(rows, "dp", [(0, 1), (1, 0)])


def turn(rows, shift):
    size = lax.axis_size("expert")
    pairs = []
    for s in range(2):
        for i in range(size):
            for d in range(2):
                j = (i + 2 * shift) % size
                pairs.append(((s * size + i) * 2 + d, (d * size + j) * 2 + s))
    return lax.ppermute(rows, ("section", "expert", "dp"), pairs)


def paired(tokens, grad_out, expert_ids, gate_probs, gate_weight, up_weight, down_weight):
    payload = pack(tokens, grad_out, expert_ids, gate_probs, gate_weight.shape[0])
    got = [turn(rows, k) for k, rows in enumerate(payload)]
    gate_weight, up_weight = pin((gate_weight, up_weight), payload[0])
    own_t, own_g = part(got)
    (down_weight,) = pin((down_weight,), own_t)
    slot_t, gate_part = gather_project([own_t] + swap_plane([own_t] * 3), gate_weight)
    gates = [gate_part, swap_dp(gate_part)]
    up_part = project(slot_t, up_weight)
    ups = [up_part, swap_dp(up_part)]
    slot_g, act_part = gather_project([own_g] + swap_plane([own_g] * 3), down_weight)
    acts = [act_part, swap_dp(act_part)]
    activation, *part_out = forward(gates, ups, down_weight)
    gate_grad, up_grad, *part_in = backward(gates, ups, acts, gate_weight, up_weight)
    grad_down = outer(slot_g, activation)
    grad_gate = outer(slot_t, gate_grad)
    grad_up = outer(slot_t, up_grad)
    sent = join(
        part_out[:1] + swap_plane(part_out[1:]), part_in[:1] + swap_plane(part_in[1:])
    )
    moe_out, grad_tokens = unpack(
        [turn(rows, -k) for k, rows in enumerate(sent)], expert_ids, gate_probs
    )
    return moe_out, grad_tokens, grad_gate, grad_up, grad_down


def solution(mesh):
    sizes = mesh.shape
    pairs = sizes["section"] == 2 and sizes["dp"] == 2 and sizes["expert"] == 2 * EXP
    return jax.shard_map(
        paired if pairs else general,
        mesh=mesh,
        in_specs=(
            P(("expert", "dp"), None),
            P(("expert", "dp"), None),
            P(("expert", "dp"), None),
            P(("expert", "dp"), None),
            P("dp", ("expert", "section")),
            P("dp", ("expert", "section")),
            P("dp", ("expert", "section")),
        ),
        out_specs=(
            P(("expert", "dp"), "section"),
            P(("expert", "dp"), "section"),
            P("dp", ("expert", "section")),
            P("dp", ("expert", "section")),
            P("dp", ("expert", "section")),
        ),
        check_vma=False,
    )
```

```python
import math

import jax
import jax.numpy as jnp
from jax import lax
from jax.experimental import pallas as pl
from jax.experimental.pallas import tpu as pltpu
from jax.sharding import PartitionSpec as P

EXP = 4
CAP = 12
BF = jnp.bfloat16
F32 = jnp.float32
TILE = 512


def contract_rows(left, right):
    return lax.dot_general(left, right, (((0,), (0,)), ((), ())), preferred_element_type=F32)


def contract_cols(left, right):
    return lax.dot_general(left, right, (((1,), (1,)), ((), ())), preferred_element_type=F32)


def slot_tables(id_match, capacity):
    chosen = jnp.any(id_match, axis=2)
    slot_rank = jnp.cumsum(chosen.astype(jnp.int32), axis=1) - 1
    slot_index = jnp.arange(capacity, dtype=jnp.int32)
    return jnp.logical_and(
        chosen[:, None, :], slot_rank[:, None, :] == slot_index[None, :, None]
    )


def general(tokens, grad_out, expert_ids, gate_probs, gate_weight, up_weight, down_weight):
    expert_devices = lax.axis_size("expert")
    model_width = tokens.shape[1]
    group_size = expert_devices // EXP
    gate_full, up_full, down_full = (
        lax.all_gather(weight, "dp", axis=0, tiled=True)
        for weight in (gate_weight, up_weight, down_weight)
    )
    own_match = expert_ids[None, :, :] == jnp.arange(EXP, dtype=jnp.int32)[:, None, None]
    own_picks = slot_tables(own_match, CAP).astype(F32)
    own_share = jnp.sum(jnp.where(own_match, gate_probs[None, :, :], 0.0), axis=2)
    own_scaled = (own_share[:, :, None] * grad_out[None].astype(F32)).astype(BF)
    pick_bf = own_picks.astype(BF)
    send_tokens = jnp.einsum("ect,td->ecd", pick_bf, tokens, preferred_element_type=F32).astype(BF)
    send_grads = jnp.einsum("ect,etd->ecd", pick_bf, own_scaled, preferred_element_type=F32).astype(BF)

    def swap(rows):
        return lax.all_to_all(rows, "expert", split_axis=0, concat_axis=0, tiled=True)

    slot_tokens = swap(jnp.repeat(send_tokens, group_size, axis=0)).reshape(-1, model_width)
    slot_grads = swap(jnp.repeat(send_grads, group_size, axis=0)).reshape(-1, model_width)
    gate_pre = jnp.dot(slot_tokens, gate_full, preferred_element_type=F32)
    up_pre = jnp.dot(slot_tokens, up_full, preferred_element_type=F32)
    act_grad = jnp.dot(slot_grads, down_full, preferred_element_type=F32)
    activation, up_grad, gate_grad = pointwise(gate_pre, up_pre, act_grad)
    partial_out = contract_cols(activation, down_full)
    partial_in = contract_cols(gate_grad, gate_full) + contract_cols(up_grad, up_full)
    summed_grads = lax.psum_scatter(
        jnp.concatenate(
            [
                contract_rows(slot_tokens, gate_grad),
                contract_rows(slot_tokens, up_grad),
                contract_rows(slot_grads, activation),
            ],
            axis=1,
        ).astype(BF),
        "dp",
        scatter_dimension=0,
        tiled=True,
    )
    hidden = gate_weight.shape[1]
    weighted_picks = own_picks * own_share[:, None, :]
    back_out = swap(partial_out.reshape(expert_devices, CAP, model_width).astype(BF)).astype(F32)
    back_in = swap(partial_in.reshape(expert_devices, CAP, model_width).astype(BF)).astype(F32)
    sum_out = back_out.reshape(EXP, group_size, CAP, model_width).sum(axis=1)
    sum_in = back_in.reshape(EXP, group_size, CAP, model_width).sum(axis=1)
    token_out = jnp.einsum("ect,ecd->td", weighted_picks, sum_out, precision=lax.Precision.HIGHEST)
    token_in = jnp.einsum("ect,ecd->td", own_picks, sum_in, precision=lax.Precision.HIGHEST)
    return (
        lax.psum_scatter(token_out.astype(BF), "section", scatter_dimension=1, tiled=True),
        lax.psum_scatter(token_in.astype(BF), "section", scatter_dimension=1, tiled=True),
        summed_grads[:, :hidden],
        summed_grads[:, hidden : 2 * hidden],
        summed_grads[:, 2 * hidden :],
    )


def pointwise(gate_pre, up_pre, act_grad):
    sigmoid_gate = jax.nn.sigmoid(gate_pre)
    silu_value = gate_pre * sigmoid_gate
    activation = (silu_value * up_pre).astype(BF)
    up_grad = (act_grad * silu_value).astype(BF)
    gate_grad = (act_grad * up_pre * sigmoid_gate * (1.0 + gate_pre * (1.0 - sigmoid_gate))).astype(BF)
    return activation, up_grad, gate_grad


def swap_expert(rows):
    size = lax.axis_size("expert")
    return lax.ppermute(rows, "expert", [(i, i ^ 1) for i in range(size)])


def swap_section(rows):
    return lax.ppermute(rows, "section", [(0, 1), (1, 0)])


def swap_plane(pieces):
    size = lax.axis_size("expert")
    both = [(s * size + i, (1 - s) * size + (i ^ 1)) for s in range(2) for i in range(size)]
    far = lax.ppermute(pieces[2], ("section", "expert"), both)
    return [swap_section(pieces[0]), swap_expert(pieces[1]), far]


ANYWHERE = pl.BlockSpec(memory_space=pl.ANY)
INSIDE = pl.BlockSpec(memory_space=pltpu.VMEM)


def params(mib):
    return pltpu.CompilerParams(vmem_limit_bytes=mib << 20)


def cost(flops, *arrays):
    moved = sum(a.size * a.dtype.itemsize for a in arrays)
    return pl.CostEstimate(flops=flops, bytes_accessed=moved, transcendentals=0)


def in_hbm(array):
    return pltpu.with_memory_space_constraint(array, pltpu.HBM)


def in_vmem(array):
    return pltpu.with_memory_space_constraint(array, pltpu.VMEM)


def pin_kernel(*refs):
    count = len(refs) // 2 - 1
    copies = [
        pltpu.make_async_copy(refs[i], refs[count + 1 + i], refs[-1].at[i]) for i in range(count)
    ]
    for copy in copies:
        copy.start()
    for copy in copies:
        copy.wait()


def pin(weights, after):
    count = len(weights)
    return pl.pallas_call(
        pin_kernel,
        out_shape=[pltpu.VMEM(weight.shape, weight.dtype) for weight in weights],
        in_specs=[ANYWHERE] * (count + 1),
        out_specs=[ANYWHERE] * count,
        scratch_shapes=[pltpu.SemaphoreType.DMA((count,))],
        cost_estimate=cost(0),
        compiler_params=params(1),
    )(*(in_hbm(weight) for weight in weights), after)


def gather_kernel(*refs):
    pieces, (w_ref, _, x_ref, out_ref) = refs[:-4][::-1], refs[-4:]
    rows = pieces[0].shape[0]
    for i, piece in enumerate(pieces):
        x_ref[i * rows : (i + 1) * rows] = piece[...]
    out_ref[...] = jnp.dot(x_ref[...], w_ref[...], preferred_element_type=F32).astype(BF)


def gather_project(pieces, weight, after):
    rows, (depth, hidden) = sum(piece.shape[0] for piece in pieces), weight.shape
    outs = [jax.ShapeDtypeStruct((rows, depth), BF), jax.ShapeDtypeStruct((rows, hidden), BF)]
    return pl.pallas_call(
        gather_kernel,
        out_shape=outs,
        in_specs=[INSIDE] * (len(pieces) + 1) + [ANYWHERE],
        out_specs=[INSIDE] * 2,
        cost_estimate=cost(0),
        compiler_params=params(14),
    )(*pieces[::-1], in_vmem(weight), after)


def project_kernel(x_ref, w_ref, out_ref):
    out_ref[...] = jnp.dot(x_ref[...], w_ref[...], preferred_element_type=F32).astype(BF)


def project(x, weight):
    rows, (depth, hidden) = x.shape[0], weight.shape
    out = jax.ShapeDtypeStruct((rows, hidden), BF)
    return pl.pallas_call(
        project_kernel,
        out_shape=out,
        in_specs=[INSIDE] * 2,
        out_specs=INSIDE,
        cost_estimate=cost(0),
        compiler_params=params(12),
    )(x, in_vmem(weight))


def iota(shape, dim):
    return lax.broadcasted_iota(jnp.int32, shape, dim)


def slot_rows(ids_ref, plane):
    count = ids_ref.shape[1]
    shape = (EXP * 2 * CAP, count)
    row = iota(shape, 0)
    place = row % (2 * CAP)
    expert = plane ^ (row // (2 * CAP))
    match = [ids_ref[j : j + 1, :] == expert for j in range(2)]
    chosen = jnp.logical_or(*match)
    before = (iota((count, count), 0) < iota((count, count), 1)).astype(F32)
    rank = jnp.dot(chosen.astype(F32), before, preferred_element_type=F32)
    picks = jnp.logical_and(chosen, rank == (place % CAP).astype(F32))
    return match, picks, place


def pack_kernel(*refs):
    hbm, out_refs, held, sem = refs[:4], refs[4 : 4 + EXP], refs[4 + EXP : 8 + EXP], refs[-1]
    half = out_refs[0].shape[1]
    cut = pl.ds(pl.multiple_of(lax.axis_index("section") * half, half), half)
    sources = [hbm[0].at[:, cut], hbm[1].at[:, cut], hbm[2], hbm[3]]
    copies = [pltpu.make_async_copy(a, b, sem.at[i]) for i, (a, b) in enumerate(zip(sources, held))]
    for copy in copies:
        copy.start()
    for copy in copies:
        copy.wait()
    tok_ref, grad_ref, ids_ref, probs_ref = held
    match, picks, place = slot_rows(ids_ref, lax.axis_index("expert") // 2)
    share = jnp.where(match[0], probs_ref[0:1, :], 0.0) + jnp.where(match[1], probs_ref[1:2, :], 0.0)
    scale = jnp.sum(jnp.where(picks, share, 0.0), axis=1, keepdims=True)
    picks = picks.astype(BF)
    tok = jnp.dot(picks, tok_ref[...], preferred_element_type=F32)
    grad = jnp.dot(picks, grad_ref[...], preferred_element_type=F32)
    payload = jnp.where(place[:, 0:1] < CAP, tok, grad * scale)
    for k, out_ref in enumerate(out_refs):
        out_ref[...] = payload[k * 2 * CAP : (k + 1) * 2 * CAP].astype(BF)


def pack(tokens, grad_out, expert_ids, gate_probs, half):
    outs = [jax.ShapeDtypeStruct((2 * CAP, half), BF)] * EXP
    rows = tokens.shape[0]
    given = (tokens, grad_out, expert_ids.T, gate_probs.T)
    return pl.pallas_call(
        pack_kernel,
        out_shape=outs,
        in_specs=[ANYWHERE] * 4,
        out_specs=[INSIDE] * EXP,
        scratch_shapes=[
            pltpu.VMEM((rows, half), BF),
            pltpu.VMEM((rows, half), BF),
            pltpu.VMEM((2, rows), jnp.int32),
            pltpu.VMEM((2, rows), F32),
            pltpu.SemaphoreType.DMA((4,)),
        ],
        cost_estimate=cost(0, tokens, grad_out, *outs),
        compiler_params=params(8),
    )(*(in_hbm(array) for array in given))


def sorting():
    n = EXP * CAP
    sorted_row, row = iota((2 * n, 2 * n), 0), iota((2 * n, 2 * n), 1)
    k, j = row // (2 * CAP), row % (2 * CAP)
    place = jnp.where(j < CAP, k * CAP + j, n + k * CAP + j - CAP)
    return (sorted_row == place).astype(BF)


def stack(refs, held_ref):
    rows = refs[0].shape[0]
    for i, ref in enumerate(refs):
        held_ref[i * rows : (i + 1) * rows] = ref[...].astype(F32)
    return held_ref[...].astype(BF)


def part_kernel(*refs):
    refs, (_, tok_ref, grad_ref, held_ref) = refs[:EXP][::-1], refs[EXP:]
    rows = jnp.dot(sorting(), stack(refs, held_ref), preferred_element_type=F32).astype(BF)
    n = EXP * CAP
    tok_ref[...] = rows[:n]
    grad_ref[...] = rows[n:]


def part(got, after):
    width = got[0].shape[1]
    outs = [jax.ShapeDtypeStruct((EXP * CAP, width), BF)] * 2
    return pl.pallas_call(
        part_kernel,
        out_shape=outs,
        in_specs=[INSIDE] * EXP + [ANYWHERE],
        out_specs=[INSIDE] * 2,
        scratch_shapes=[pltpu.VMEM((2 * EXP * CAP, width), F32)],
        cost_estimate=cost(0, *got, *outs),
        compiler_params=params(8),
    )(*got[::-1], after)


def join_kernel(*refs):
    outs, ins, sent = refs[:4], refs[4:8], refs[8:]

    def total(pieces):
        return sum(p[...].astype(F32) for p in pieces).astype(BF)

    rows = jnp.concatenate([total(outs), total(ins)], axis=0)
    rows = lax.dot_general(
        sorting(), rows, (((0,), (0,)), ((), ())), preferred_element_type=F32
    )
    for k, ref in enumerate(sent):
        ref[...] = rows[k * 2 * CAP : (k + 1) * 2 * CAP].astype(BF)


def join(outs, ins):
    width = outs[0].shape[1]
    sent = [jax.ShapeDtypeStruct((2 * CAP, width), BF)] * EXP
    return pl.pallas_call(
        join_kernel,
        out_shape=sent,
        in_specs=[INSIDE] * 8,
        out_specs=[INSIDE] * EXP,
        cost_estimate=cost(0, *outs, *ins, *sent),
        compiler_params=params(10),
    )(*outs[::-1], *ins[::-1])


def unpack_kernel(*refs):
    refs, (ids_ref, probs_ref, out_ref, in_ref, held_ref) = refs[:EXP][::-1], refs[EXP:]
    match, picks, place = slot_rows(ids_ref, lax.axis_index("expert") // 2)
    rows = stack(refs, held_ref)
    count = ids_ref.shape[1]
    same = iota((count, count), 0) == iota((count, count), 1)
    probs = [
        jnp.sum(jnp.where(same, probs_ref[j : j + 1, :], 0.0), axis=1, keepdims=True)
        for j in range(2)
    ]

    def found(where):
        return contract_rows(jnp.logical_and(picks, where).astype(BF), rows)

    first = place < CAP
    out_ref[...] = (
        probs[0] * found(jnp.logical_and(first, match[0]))
        + probs[1] * found(jnp.logical_and(first, match[1]))
    ).astype(BF)
    in_ref[...] = found(jnp.logical_not(first)).astype(BF)


def unpack(back, expert_ids, gate_probs):
    width = back[0].shape[1]
    outs = [jax.ShapeDtypeStruct((expert_ids.shape[0], width), BF)] * 2
    return pl.pallas_call(
        unpack_kernel,
        out_shape=outs,
        in_specs=[INSIDE] * (EXP + 2),
        out_specs=[INSIDE] * 2,
        scratch_shapes=[pltpu.VMEM((2 * EXP * CAP, width), F32)],
        cost_estimate=cost(0, *back, *outs),
        compiler_params=params(8),
    )(*back[::-1], expert_ids.T, gate_probs.T)


def spread(rows, refs):
    count = refs[0].shape[0]
    for i, ref in enumerate(refs):
        ref[...] = rows[i * count : (i + 1) * count].astype(BF)


def times_rows(lefts, weights, turned, refs):
    depth = weights[0].shape[0]
    tile = math.gcd(depth, TILE)
    for left, held in zip(lefts, turned):
        held[...] = left[...].T
    for at in range(0, depth, tile):
        cut = slice(at, at + tile)
        spread(
            sum(
                jnp.dot(weight[cut], held[...], preferred_element_type=F32)
                for weight, held in zip(weights, turned)
            )
            .astype(BF)
            .T,
            refs,
            cut,
        )


def spread(rows, refs, cut):
    count = refs[0].shape[0]
    for i, ref in enumerate(refs):
        ref[:, cut] = rows[i * count : (i + 1) * count]


def forward_kernel(g0_ref, g1_ref, u0_ref, u1_ref, w_ref, act_ref, silu_ref, slope_ref, *refs):
    hidden = act_ref.shape[1]
    tile = math.gcd(hidden, TILE)
    for at in range(0, hidden, tile):
        cut = slice(at, at + tile)
        gate_pre = g0_ref[:, cut].astype(F32) + g1_ref[:, cut].astype(F32)
        up_pre = u0_ref[:, cut].astype(F32) + u1_ref[:, cut].astype(F32)
        sigmoid_gate = jax.nn.sigmoid(gate_pre)
        silu_value = gate_pre * sigmoid_gate
        act_ref[:, cut] = (silu_value * up_pre).astype(BF)
        silu_ref[:, cut] = silu_value
        slope_ref[:, cut] = up_pre * sigmoid_gate * (1.0 + gate_pre * (1.0 - sigmoid_gate))
    times_rows([act_ref], [w_ref], refs[4:], refs[:4])


def forward(gates, ups, weight):
    rows, (depth, hidden) = gates[0].shape[0], weight.shape
    outs = [jax.ShapeDtypeStruct((rows, hidden), BF)]
    outs += [jax.ShapeDtypeStruct((rows, hidden), F32)] * 2
    outs += [jax.ShapeDtypeStruct((rows // 4, depth), BF)] * 4
    return pl.pallas_call(
        forward_kernel,
        out_shape=outs,
        in_specs=[INSIDE] * 5,
        out_specs=[INSIDE] * 7,
        scratch_shapes=[pltpu.VMEM((hidden, rows), BF)],
        cost_estimate=cost(0),
        compiler_params=params(18),
    )(*gates, *ups, in_vmem(weight))


def backward_kernel(
    a0_ref, a1_ref, silu_ref, slope_ref, wg_ref, wu_ref, dg_ref, du_ref, *refs
):
    hidden = dg_ref.shape[1]
    tile = math.gcd(hidden, TILE)
    for at in range(0, hidden, tile):
        cut = slice(at, at + tile)
        act_grad = a0_ref[:, cut].astype(F32) + a1_ref[:, cut].astype(F32)
        dg_ref[:, cut] = (act_grad * slope_ref[:, cut]).astype(BF)
        du_ref[:, cut] = (act_grad * silu_ref[:, cut]).astype(BF)
    times_rows([dg_ref, du_ref], [wg_ref, wu_ref], refs[4:], refs[:4])


def backward(acts, silu_value, slope, gate_weight, up_weight):
    rows, (depth, hidden) = acts[0].shape[0], gate_weight.shape
    outs = [jax.ShapeDtypeStruct((rows, hidden), BF)] * 2
    outs += [jax.ShapeDtypeStruct((rows // 4, depth), BF)] * 4
    return pl.pallas_call(
        backward_kernel,
        out_shape=outs,
        in_specs=[INSIDE] * 6,
        out_specs=[INSIDE] * 6,
        scratch_shapes=[pltpu.VMEM((hidden, rows), BF)] * 2,
        cost_estimate=cost(4 * rows * depth * hidden, *acts, silu_value, slope, *outs),
        compiler_params=params(20),
    )(*acts, silu_value, slope, in_vmem(gate_weight), in_vmem(up_weight))


def outer_kernel(x_ref, y_ref, out_ref, turned_ref, held_ref, sem):
    depth = held_ref.shape[0]
    tile = math.gcd(depth, 256)
    turned_ref[...] = x_ref[...].T
    copies = []
    for i, at in enumerate(range(0, depth, tile)):
        cut = slice(at, at + tile)
        held_ref[cut] = jnp.dot(
            turned_ref[cut], y_ref[...], preferred_element_type=F32
        ).astype(BF)
        copies.append(pltpu.make_async_copy(held_ref.at[cut], out_ref.at[cut], sem.at[i]))
        copies[-1].start()
    for copy in copies:
        copy.wait()


def outer(x, y):
    (rows, depth), hidden = x.shape, y.shape[1]
    out = jax.ShapeDtypeStruct((depth, hidden), BF)
    return pl.pallas_call(
        outer_kernel,
        out_shape=out,
        in_specs=[INSIDE] * 2,
        out_specs=ANYWHERE,
        scratch_shapes=[
            pltpu.VMEM((depth, rows), BF),
            pltpu.VMEM((depth, hidden), BF),
            pltpu.SemaphoreType.DMA((depth // math.gcd(depth, 256),)),
        ],
        cost_estimate=cost(2 * rows * depth * hidden, x, y, out),
        compiler_params=params(24),
    )(x, y)


def swap_dp(rows):
    return lax.ppermute(rows, "dp", [(0, 1), (1, 0)])


def turn(pieces):
    size = lax.axis_size("expert")
    got = {}
    for k in reversed(range(EXP)):
        pairs = [
            ((s * size + i) * 2 + d, (d * size + (i ^ (2 * k))) * 2 + s)
            for s in range(2)
            for i in range(size)
            for d in range(2)
        ]
        got[k] = lax.ppermute(pieces[k], ("section", "expert", "dp"), pairs)
    return [got[k] for k in range(EXP)]


def paired(tokens, grad_out, expert_ids, gate_probs, gate_weight, up_weight, down_weight):
    payload = pack(tokens, grad_out, expert_ids, gate_probs, gate_weight.shape[0])
    got = turn(payload)
    gate_weight, up_weight = pin((gate_weight, up_weight), payload[0])
    own_t, own_g = part(got, gate_weight)
    (down_weight,) = pin((down_weight,), own_t)
    slot_t, gate_part = gather_project([own_t] + swap_plane([own_t] * 3), gate_weight, down_weight)
    gates = [gate_part, swap_dp(gate_part)]
    up_part = project(slot_t, up_weight)
    ups = [up_part, swap_dp(up_part)]
    activation, silu_value, slope, *part_out = forward(gates, ups, down_weight)
    slot_g, act_part = gather_project(
        [own_g] + swap_plane([own_g] * 3), down_weight, up_part
    )
    acts = [act_part, swap_dp(act_part)]
    part_out, _ = lax.optimization_barrier((part_out, act_part))
    gate_grad, up_grad, *part_in = backward(acts, silu_value, slope, gate_weight, up_weight)
    grad_down = outer(slot_g, activation)
    grad_gate = outer(slot_t, gate_grad)
    grad_up = outer(slot_t, up_grad)
    sent = join(
        part_out[:1] + swap_plane(part_out[1:]), part_in[:1] + swap_plane(part_in[1:])
    )
    moe_out, grad_tokens = unpack(turn(sent), expert_ids, gate_probs)
    return moe_out, grad_tokens, grad_gate, grad_up, grad_down


def solution(mesh):
    sizes = mesh.shape
    pairs = sizes["section"] == 2 and sizes["dp"] == 2 and sizes["expert"] == 2 * EXP
    return jax.shard_map(
        paired if pairs else general,
        mesh=mesh,
        in_specs=(
            P(("expert", "dp"), None),
            P(("expert", "dp"), None),
            P(("expert", "dp"), None),
            P(("expert", "dp"), None),
            P("dp", ("expert", "section")),
            P("dp", ("expert", "section")),
            P("dp", ("expert", "section")),
        ),
        out_specs=(
            P(("expert", "dp"), "section"),
            P(("expert", "dp"), "section"),
            P("dp", ("expert", "section")),
            P("dp", ("expert", "section")),
            P("dp", ("expert", "section")),
        ),
        check_vma=False,
    )
```

```python
import math

import jax
import jax.numpy as jnp
from jax import lax
from jax.experimental import pallas as pl
from jax.experimental.pallas import tpu as pltpu
from jax.sharding import PartitionSpec as P

EXP = 4
CAP = 12
BF = jnp.bfloat16
F32 = jnp.float32
TILE = 256


def contract_rows(left, right):
    return lax.dot_general(left, right, (((0,), (0,)), ((), ())), preferred_element_type=F32)


def contract_cols(left, right):
    return lax.dot_general(left, right, (((1,), (1,)), ((), ())), preferred_element_type=F32)


def slot_tables(id_match, capacity):
    chosen = jnp.any(id_match, axis=2)
    slot_rank = jnp.cumsum(chosen.astype(jnp.int32), axis=1) - 1
    slot_index = jnp.arange(capacity, dtype=jnp.int32)
    return jnp.logical_and(
        chosen[:, None, :], slot_rank[:, None, :] == slot_index[None, :, None]
    )


def general(tokens, grad_out, expert_ids, gate_probs, gate_weight, up_weight, down_weight):
    expert_devices = lax.axis_size("expert")
    model_width = tokens.shape[1]
    group_size = expert_devices // EXP
    gate_full, up_full, down_full = (
        lax.all_gather(weight, "dp", axis=0, tiled=True)
        for weight in (gate_weight, up_weight, down_weight)
    )
    own_match = expert_ids[None, :, :] == jnp.arange(EXP, dtype=jnp.int32)[:, None, None]
    own_picks = slot_tables(own_match, CAP).astype(F32)
    own_share = jnp.sum(jnp.where(own_match, gate_probs[None, :, :], 0.0), axis=2)
    own_scaled = (own_share[:, :, None] * grad_out[None].astype(F32)).astype(BF)
    pick_bf = own_picks.astype(BF)
    send_tokens = jnp.einsum("ect,td->ecd", pick_bf, tokens, preferred_element_type=F32).astype(BF)
    send_grads = jnp.einsum("ect,etd->ecd", pick_bf, own_scaled, preferred_element_type=F32).astype(BF)

    def swap(rows):
        return lax.all_to_all(rows, "expert", split_axis=0, concat_axis=0, tiled=True)

    slot_tokens = swap(jnp.repeat(send_tokens, group_size, axis=0)).reshape(-1, model_width)
    slot_grads = swap(jnp.repeat(send_grads, group_size, axis=0)).reshape(-1, model_width)
    gate_pre = jnp.dot(slot_tokens, gate_full, preferred_element_type=F32)
    up_pre = jnp.dot(slot_tokens, up_full, preferred_element_type=F32)
    act_grad = jnp.dot(slot_grads, down_full, preferred_element_type=F32)
    activation, up_grad, gate_grad = pointwise(gate_pre, up_pre, act_grad)
    partial_out = contract_cols(activation, down_full)
    partial_in = contract_cols(gate_grad, gate_full) + contract_cols(up_grad, up_full)
    summed_grads = lax.psum_scatter(
        jnp.concatenate(
            [
                contract_rows(slot_tokens, gate_grad),
                contract_rows(slot_tokens, up_grad),
                contract_rows(slot_grads, activation),
            ],
            axis=1,
        ).astype(BF),
        "dp",
        scatter_dimension=0,
        tiled=True,
    )
    hidden = gate_weight.shape[1]
    weighted_picks = own_picks * own_share[:, None, :]
    back_out = swap(partial_out.reshape(expert_devices, CAP, model_width).astype(BF)).astype(F32)
    back_in = swap(partial_in.reshape(expert_devices, CAP, model_width).astype(BF)).astype(F32)
    sum_out = back_out.reshape(EXP, group_size, CAP, model_width).sum(axis=1)
    sum_in = back_in.reshape(EXP, group_size, CAP, model_width).sum(axis=1)
    token_out = jnp.einsum("ect,ecd->td", weighted_picks, sum_out, precision=lax.Precision.HIGHEST)
    token_in = jnp.einsum("ect,ecd->td", own_picks, sum_in, precision=lax.Precision.HIGHEST)
    return (
        lax.psum_scatter(token_out.astype(BF), "section", scatter_dimension=1, tiled=True),
        lax.psum_scatter(token_in.astype(BF), "section", scatter_dimension=1, tiled=True),
        summed_grads[:, :hidden],
        summed_grads[:, hidden : 2 * hidden],
        summed_grads[:, 2 * hidden :],
    )


def pointwise(gate_pre, up_pre, act_grad):
    sigmoid_gate = jax.nn.sigmoid(gate_pre)
    silu_value = gate_pre * sigmoid_gate
    activation = (silu_value * up_pre).astype(BF)
    up_grad = (act_grad * silu_value).astype(BF)
    gate_grad = (act_grad * up_pre * sigmoid_gate * (1.0 + gate_pre * (1.0 - sigmoid_gate))).astype(BF)
    return activation, up_grad, gate_grad


def swap_expert(rows):
    size = lax.axis_size("expert")
    return lax.ppermute(rows, "expert", [(i, i ^ 1) for i in range(size)])


def swap_section(rows):
    return lax.ppermute(rows, "section", [(0, 1), (1, 0)])


def swap_plane(pieces):
    size = lax.axis_size("expert")
    both = [(s * size + i, (1 - s) * size + (i ^ 1)) for s in range(2) for i in range(size)]
    far = lax.ppermute(pieces[2], ("section", "expert"), both)
    return [swap_section(pieces[0]), swap_expert(pieces[1]), far]


ANYWHERE = pl.BlockSpec(memory_space=pl.ANY)
INSIDE = pl.BlockSpec(memory_space=pltpu.VMEM)


def params(mib):
    return pltpu.CompilerParams(vmem_limit_bytes=mib << 20)


def cost(flops, *arrays):
    moved = sum(a.size * a.dtype.itemsize for a in arrays)
    return pl.CostEstimate(flops=flops, bytes_accessed=moved, transcendentals=0)


def in_hbm(array):
    return pltpu.with_memory_space_constraint(array, pltpu.HBM)


def in_vmem(array):
    return pltpu.with_memory_space_constraint(array, pltpu.VMEM)


def pin_kernel(*refs):
    count = len(refs) // 2 - 1
    copies = [
        pltpu.make_async_copy(refs[i], refs[count + 1 + i], refs[-1].at[i]) for i in range(count)
    ]
    for copy in copies:
        copy.start()
    for copy in copies:
        copy.wait()


def pin(weights, after):
    count = len(weights)
    return pl.pallas_call(
        pin_kernel,
        out_shape=[pltpu.VMEM(weight.shape, weight.dtype) for weight in weights],
        in_specs=[ANYWHERE] * (count + 1),
        out_specs=[ANYWHERE] * count,
        scratch_shapes=[pltpu.SemaphoreType.DMA((count,))],
        cost_estimate=cost(0),
        compiler_params=params(1),
    )(*(in_hbm(weight) for weight in weights), after)


def gather_kernel(*refs):
    pieces, (w_ref, _, x_ref, out_ref) = refs[:-4][::-1], refs[-4:]
    rows = pieces[0].shape[0]
    for i, piece in enumerate(pieces):
        x_ref[i * rows : (i + 1) * rows] = piece[...]
    out_ref[...] = jnp.dot(x_ref[...], w_ref[...], preferred_element_type=F32).astype(BF)


def gather_project(pieces, weight, after):
    rows, (depth, hidden) = sum(piece.shape[0] for piece in pieces), weight.shape
    outs = [jax.ShapeDtypeStruct((rows, depth), BF), jax.ShapeDtypeStruct((rows, hidden), BF)]
    return pl.pallas_call(
        gather_kernel,
        out_shape=outs,
        in_specs=[INSIDE] * (len(pieces) + 1) + [ANYWHERE],
        out_specs=[INSIDE] * 2,
        cost_estimate=cost(0),
        compiler_params=params(14),
    )(*pieces[::-1], in_vmem(weight), after)


def project_kernel(x_ref, w_ref, out_ref):
    out_ref[...] = jnp.dot(x_ref[...], w_ref[...], preferred_element_type=F32).astype(BF)


def project(x, weight):
    rows, (depth, hidden) = x.shape[0], weight.shape
    out = jax.ShapeDtypeStruct((rows, hidden), BF)
    return pl.pallas_call(
        project_kernel,
        out_shape=out,
        in_specs=[INSIDE] * 2,
        out_specs=INSIDE,
        cost_estimate=cost(0),
        compiler_params=params(12),
    )(x, in_vmem(weight))


def iota(shape, dim):
    return lax.broadcasted_iota(jnp.int32, shape, dim)


def slot_rows(ids_ref, plane):
    count = ids_ref.shape[1]
    shape = (EXP * 2 * CAP, count)
    row = iota(shape, 0)
    place = row % (2 * CAP)
    expert = plane ^ (row // (2 * CAP))
    match = [ids_ref[j : j + 1, :] == expert for j in range(2)]
    chosen = jnp.logical_or(*match)
    before = (iota((count, count), 0) < iota((count, count), 1)).astype(F32)
    rank = jnp.dot(chosen.astype(F32), before, preferred_element_type=F32)
    picks = jnp.logical_and(chosen, rank == (place % CAP).astype(F32))
    return match, picks, place


def pack_kernel(*refs):
    hbm, out_refs, held, sem = refs[:4], refs[4 : 4 + EXP], refs[4 + EXP : 8 + EXP], refs[-1]
    half = out_refs[0].shape[1]
    cut = pl.ds(pl.multiple_of(lax.axis_index("section") * half, half), half)
    sources = [hbm[0].at[:, cut], hbm[1].at[:, cut], hbm[2], hbm[3]]
    copies = [pltpu.make_async_copy(a, b, sem.at[i]) for i, (a, b) in enumerate(zip(sources, held))]
    for copy in copies:
        copy.start()
    for copy in copies:
        copy.wait()
    tok_ref, grad_ref, ids_ref, probs_ref = held
    match, picks, place = slot_rows(ids_ref, lax.axis_index("expert") // 2)
    share = jnp.where(match[0], probs_ref[0:1, :], 0.0) + jnp.where(match[1], probs_ref[1:2, :], 0.0)
    scale = jnp.sum(jnp.where(picks, share, 0.0), axis=1, keepdims=True)
    picks = picks.astype(BF)
    tok = jnp.dot(picks, tok_ref[...], preferred_element_type=F32)
    grad = jnp.dot(picks, grad_ref[...], preferred_element_type=F32)
    payload = jnp.where(place[:, 0:1] < CAP, tok, grad * scale)
    for k, out_ref in enumerate(out_refs):
        out_ref[...] = payload[k * 2 * CAP : (k + 1) * 2 * CAP].astype(BF)


def pack(tokens, grad_out, expert_ids, gate_probs, half):
    outs = [jax.ShapeDtypeStruct((2 * CAP, half), BF)] * EXP
    rows = tokens.shape[0]
    given = (tokens, grad_out, expert_ids.T, gate_probs.T)
    return pl.pallas_call(
        pack_kernel,
        out_shape=outs,
        in_specs=[ANYWHERE] * 4,
        out_specs=[INSIDE] * EXP,
        scratch_shapes=[
            pltpu.VMEM((rows, half), BF),
            pltpu.VMEM((rows, half), BF),
            pltpu.VMEM((2, rows), jnp.int32),
            pltpu.VMEM((2, rows), F32),
            pltpu.SemaphoreType.DMA((4,)),
        ],
        cost_estimate=cost(0, tokens, grad_out, *outs),
        compiler_params=params(8),
    )(*(in_hbm(array) for array in given))


def sorting():
    n = EXP * CAP
    sorted_row, row = iota((2 * n, 2 * n), 0), iota((2 * n, 2 * n), 1)
    k, j = row // (2 * CAP), row % (2 * CAP)
    place = jnp.where(j < CAP, k * CAP + j, n + k * CAP + j - CAP)
    return (sorted_row == place).astype(BF)


def stack(refs, held_ref):
    rows = refs[0].shape[0]
    for i, ref in enumerate(refs):
        held_ref[i * rows : (i + 1) * rows] = ref[...].astype(F32)
    return held_ref[...].astype(BF)


def part_kernel(*refs):
    refs, (_, tok_ref, grad_ref, held_ref) = refs[:EXP][::-1], refs[EXP:]
    rows = jnp.dot(sorting(), stack(refs, held_ref), preferred_element_type=F32).astype(BF)
    n = EXP * CAP
    tok_ref[...] = rows[:n]
    grad_ref[...] = rows[n:]


def part(got, after):
    width = got[0].shape[1]
    outs = [jax.ShapeDtypeStruct((EXP * CAP, width), BF)] * 2
    return pl.pallas_call(
        part_kernel,
        out_shape=outs,
        in_specs=[INSIDE] * EXP + [ANYWHERE],
        out_specs=[INSIDE] * 2,
        scratch_shapes=[pltpu.VMEM((2 * EXP * CAP, width), F32)],
        cost_estimate=cost(0, *got, *outs),
        compiler_params=params(8),
    )(*got[::-1], after)


def join_kernel(*refs):
    outs, ins, sent = refs[:4], refs[4:8], refs[8:]

    def total(pieces):
        return sum(p[...].astype(F32) for p in pieces).astype(BF)

    rows = jnp.concatenate([total(outs), total(ins)], axis=0)
    rows = lax.dot_general(
        sorting(), rows, (((0,), (0,)), ((), ())), preferred_element_type=F32
    )
    for k, ref in enumerate(sent):
        ref[...] = rows[k * 2 * CAP : (k + 1) * 2 * CAP].astype(BF)


def join(outs, ins):
    width = outs[0].shape[1]
    sent = [jax.ShapeDtypeStruct((2 * CAP, width), BF)] * EXP
    return pl.pallas_call(
        join_kernel,
        out_shape=sent,
        in_specs=[INSIDE] * 8,
        out_specs=[INSIDE] * EXP,
        cost_estimate=cost(0, *outs, *ins, *sent),
        compiler_params=params(10),
    )(*outs[::-1], *ins[::-1])


def unpack_kernel(*refs):
    refs, (ids_ref, probs_ref, out_ref, in_ref, held_ref) = refs[:EXP][::-1], refs[EXP:]
    match, picks, place = slot_rows(ids_ref, lax.axis_index("expert") // 2)
    rows = stack(refs, held_ref)
    count = ids_ref.shape[1]
    same = iota((count, count), 0) == iota((count, count), 1)
    probs = [
        jnp.sum(jnp.where(same, probs_ref[j : j + 1, :], 0.0), axis=1, keepdims=True)
        for j in range(2)
    ]

    def found(where):
        return contract_rows(jnp.logical_and(picks, where).astype(BF), rows)

    first = place < CAP
    out_ref[...] = (
        probs[0] * found(jnp.logical_and(first, match[0]))
        + probs[1] * found(jnp.logical_and(first, match[1]))
    ).astype(BF)
    in_ref[...] = found(jnp.logical_not(first)).astype(BF)


def unpack(back, expert_ids, gate_probs):
    width = back[0].shape[1]
    outs = [jax.ShapeDtypeStruct((expert_ids.shape[0], width), BF)] * 2
    return pl.pallas_call(
        unpack_kernel,
        out_shape=outs,
        in_specs=[INSIDE] * (EXP + 2),
        out_specs=[INSIDE] * 2,
        scratch_shapes=[pltpu.VMEM((2 * EXP * CAP, width), F32)],
        cost_estimate=cost(0, *back, *outs),
        compiler_params=params(8),
    )(*back[::-1], expert_ids.T, gate_probs.T)


def spread(rows, refs):
    count = refs[0].shape[0]
    for i, ref in enumerate(refs):
        ref[...] = rows[i * count : (i + 1) * count].astype(BF)


def times_rows(lefts, weights, turned, refs):
    depth = weights[0].shape[0]
    tile = math.gcd(depth, TILE)
    for left, held in zip(lefts, turned):
        held[...] = left[...].T
    for at in range(0, depth, tile):
        cut = slice(at, at + tile)
        spread(
            sum(
                jnp.dot(weight[cut], held[...], preferred_element_type=F32)
                for weight, held in zip(weights, turned)
            )
            .astype(BF)
            .T,
            refs,
            cut,
        )


def spread(rows, refs, cut):
    count = refs[0].shape[0]
    for i, ref in enumerate(refs):
        ref[:, cut] = rows[i * count : (i + 1) * count]


def forward_kernel(g0_ref, g1_ref, u0_ref, u1_ref, w_ref, act_ref, silu_ref, slope_ref, *refs):
    hidden = act_ref.shape[1]
    tile = math.gcd(hidden, TILE)
    for at in range(0, hidden, tile):
        cut = slice(at, at + tile)
        gate_pre = g0_ref[:, cut].astype(F32) + g1_ref[:, cut].astype(F32)
        up_pre = u0_ref[:, cut].astype(F32) + u1_ref[:, cut].astype(F32)
        sigmoid_gate = jax.nn.sigmoid(gate_pre)
        silu_value = gate_pre * sigmoid_gate
        act_ref[:, cut] = (silu_value * up_pre).astype(BF)
        silu_ref[:, cut] = silu_value
        slope_ref[:, cut] = up_pre * sigmoid_gate * (1.0 + gate_pre * (1.0 - sigmoid_gate))
    times_rows([act_ref], [w_ref], refs[4:], refs[:4])


def forward(gates, ups, weight):
    rows, (depth, hidden) = gates[0].shape[0], weight.shape
    outs = [jax.ShapeDtypeStruct((rows, hidden), BF)]
    outs += [jax.ShapeDtypeStruct((rows, hidden), F32)] * 2
    outs += [jax.ShapeDtypeStruct((rows // 4, depth), BF)] * 4
    return pl.pallas_call(
        forward_kernel,
        out_shape=outs,
        in_specs=[INSIDE] * 5,
        out_specs=[INSIDE] * 7,
        scratch_shapes=[pltpu.VMEM((hidden, rows), BF)],
        cost_estimate=cost(0),
        compiler_params=params(18),
    )(*gates, *ups, in_vmem(weight))


def backward_kernel(
    a0_ref, a1_ref, silu_ref, slope_ref, wg_ref, wu_ref, dg_ref, du_ref, *refs
):
    hidden = dg_ref.shape[1]
    tile = math.gcd(hidden, TILE)
    for at in range(0, hidden, tile):
        cut = slice(at, at + tile)
        act_grad = a0_ref[:, cut].astype(F32) + a1_ref[:, cut].astype(F32)
        dg_ref[:, cut] = (act_grad * slope_ref[:, cut]).astype(BF)
        du_ref[:, cut] = (act_grad * silu_ref[:, cut]).astype(BF)
    times_rows([dg_ref, du_ref], [wg_ref, wu_ref], refs[4:], refs[:4])


def backward(acts, silu_value, slope, gate_weight, up_weight):
    rows, (depth, hidden) = acts[0].shape[0], gate_weight.shape
    outs = [jax.ShapeDtypeStruct((rows, hidden), BF)] * 2
    outs += [jax.ShapeDtypeStruct((rows // 4, depth), BF)] * 4
    return pl.pallas_call(
        backward_kernel,
        out_shape=outs,
        in_specs=[INSIDE] * 6,
        out_specs=[INSIDE] * 6,
        scratch_shapes=[pltpu.VMEM((hidden, rows), BF)] * 2,
        cost_estimate=cost(4 * rows * depth * hidden, *acts, silu_value, slope, *outs),
        compiler_params=params(20),
    )(*acts, silu_value, slope, in_vmem(gate_weight), in_vmem(up_weight))


def outer_kernel(*refs):
    count = (len(refs) - 4) // 2
    x_ref, y_refs, out_refs = refs[0], refs[1 : 1 + count], refs[1 + count : 1 + 2 * count]
    turned_ref, held_ref, sem = refs[-3:]
    depth = held_ref.shape[1]
    tile = math.gcd(depth, 256)
    turned_ref[...] = x_ref[...].T
    copies = []
    for j in range(count):
        for i, at in enumerate(range(0, depth, tile)):
            cut = slice(at, at + tile)
            held_ref[j, cut] = jnp.dot(
                turned_ref[cut], y_refs[j][...], preferred_element_type=F32
            ).astype(BF)
            copies.append(
                pltpu.make_async_copy(held_ref.at[j, cut], out_refs[j].at[cut], sem.at[j, i])
            )
            copies[-1].start()
    for copy in copies:
        copy.wait()


def outer(x, *ys):
    (rows, depth), hidden, count = x.shape, ys[0].shape[1], len(ys)
    outs = [jax.ShapeDtypeStruct((depth, hidden), BF)] * count
    return pl.pallas_call(
        outer_kernel,
        out_shape=outs,
        in_specs=[INSIDE] * (1 + count),
        out_specs=[ANYWHERE] * count,
        scratch_shapes=[
            pltpu.VMEM((depth, rows), BF),
            pltpu.VMEM((count, depth, hidden), BF),
            pltpu.SemaphoreType.DMA((count, depth // math.gcd(depth, 256))),
        ],
        cost_estimate=cost(2 * rows * depth * hidden * count, x, *ys, *outs),
        compiler_params=params(20 + 8 * count),
    )(x, *ys)


def swap_dp(rows):
    return lax.ppermute(rows, "dp", [(0, 1), (1, 0)])


def turn(pieces):
    size = lax.axis_size("expert")
    got = {}
    for k in reversed(range(EXP)):
        pairs = [
            ((s * size + i) * 2 + d, (d * size + (i ^ (2 * k))) * 2 + s)
            for s in range(2)
            for i in range(size)
            for d in range(2)
        ]
        got[k] = lax.ppermute(pieces[k], ("section", "expert", "dp"), pairs)
    return [got[k] for k in range(EXP)]


def paired(tokens, grad_out, expert_ids, gate_probs, gate_weight, up_weight, down_weight):
    payload = pack(tokens, grad_out, expert_ids, gate_probs, gate_weight.shape[0])
    got = turn(payload)
    (gate_weight,) = pin((gate_weight,), payload[0])
    own_t, own_g = part(got, gate_weight)

    slot_t, gate_part = gather_project([own_t] + swap_plane([own_t] * 3), gate_weight, own_t)
    gates = [gate_part, swap_dp(gate_part)]
    up_part = project(slot_t, up_weight)
    ups = [up_part, swap_dp(up_part)]
    activation, silu_value, slope, *part_out = forward(gates, ups, down_weight)
    slot_g, act_part = gather_project(
        [own_g] + swap_plane([own_g] * 3), down_weight, up_part
    )
    acts = [act_part, swap_dp(act_part)]
    part_out, _ = lax.optimization_barrier((part_out, act_part))
    gate_grad, up_grad, *part_in = backward(acts, silu_value, slope, gate_weight, up_weight)
    (grad_down,) = outer(slot_g, activation)
    grad_gate, grad_up = outer(slot_t, gate_grad, up_grad)
    sent = join(
        part_out[:1] + swap_plane(part_out[1:]), part_in[:1] + swap_plane(part_in[1:])
    )
    moe_out, grad_tokens = unpack(turn(sent), expert_ids, gate_probs)
    return moe_out, grad_tokens, grad_gate, grad_up, grad_down


def solution(mesh):
    sizes = mesh.shape
    pairs = sizes["section"] == 2 and sizes["dp"] == 2 and sizes["expert"] == 2 * EXP
    return jax.shard_map(
        paired if pairs else general,
        mesh=mesh,
        in_specs=(
            P(("expert", "dp"), None),
            P(("expert", "dp"), None),
            P(("expert", "dp"), None),
            P(("expert", "dp"), None),
            P("dp", ("expert", "section")),
            P("dp", ("expert", "section")),
            P("dp", ("expert", "section")),
        ),
        out_specs=(
            P(("expert", "dp"), "section"),
            P(("expert", "dp"), "section"),
            P("dp", ("expert", "section")),
            P("dp", ("expert", "section")),
            P("dp", ("expert", "section")),
        ),
        check_vma=False,
    )
```

```python
import math

import jax
import jax.numpy as jnp
from jax import lax
from jax.experimental import pallas as pl
from jax.experimental.pallas import tpu as pltpu
from jax.sharding import PartitionSpec as P

EXP = 4
CAP = 12
BF = jnp.bfloat16
F32 = jnp.float32
TILE = 256


def contract_rows(left, right):
    return lax.dot_general(left, right, (((0,), (0,)), ((), ())), preferred_element_type=F32)


def contract_cols(left, right):
    return lax.dot_general(left, right, (((1,), (1,)), ((), ())), preferred_element_type=F32)


def slot_tables(id_match, capacity):
    chosen = jnp.any(id_match, axis=2)
    slot_rank = jnp.cumsum(chosen.astype(jnp.int32), axis=1) - 1
    slot_index = jnp.arange(capacity, dtype=jnp.int32)
    return jnp.logical_and(
        chosen[:, None, :], slot_rank[:, None, :] == slot_index[None, :, None]
    )


def general(tokens, grad_out, expert_ids, gate_probs, gate_weight, up_weight, down_weight):
    expert_devices = lax.axis_size("expert")
    model_width = tokens.shape[1]
    group_size = expert_devices // EXP
    gate_full, up_full, down_full = (
        lax.all_gather(weight, "dp", axis=0, tiled=True)
        for weight in (gate_weight, up_weight, down_weight)
    )
    own_match = expert_ids[None, :, :] == jnp.arange(EXP, dtype=jnp.int32)[:, None, None]
    own_picks = slot_tables(own_match, CAP).astype(F32)
    own_share = jnp.sum(jnp.where(own_match, gate_probs[None, :, :], 0.0), axis=2)
    own_scaled = (own_share[:, :, None] * grad_out[None].astype(F32)).astype(BF)
    pick_bf = own_picks.astype(BF)
    send_tokens = jnp.einsum("ect,td->ecd", pick_bf, tokens, preferred_element_type=F32).astype(BF)
    send_grads = jnp.einsum("ect,etd->ecd", pick_bf, own_scaled, preferred_element_type=F32).astype(BF)

    def swap(rows):
        return lax.all_to_all(rows, "expert", split_axis=0, concat_axis=0, tiled=True)

    slot_tokens = swap(jnp.repeat(send_tokens, group_size, axis=0)).reshape(-1, model_width)
    slot_grads = swap(jnp.repeat(send_grads, group_size, axis=0)).reshape(-1, model_width)
    gate_pre = jnp.dot(slot_tokens, gate_full, preferred_element_type=F32)
    up_pre = jnp.dot(slot_tokens, up_full, preferred_element_type=F32)
    act_grad = jnp.dot(slot_grads, down_full, preferred_element_type=F32)
    activation, up_grad, gate_grad = pointwise(gate_pre, up_pre, act_grad)
    partial_out = contract_cols(activation, down_full)
    partial_in = contract_cols(gate_grad, gate_full) + contract_cols(up_grad, up_full)
    summed_grads = lax.psum_scatter(
        jnp.concatenate(
            [
                contract_rows(slot_tokens, gate_grad),
                contract_rows(slot_tokens, up_grad),
                contract_rows(slot_grads, activation),
            ],
            axis=1,
        ).astype(BF),
        "dp",
        scatter_dimension=0,
        tiled=True,
    )
    hidden = gate_weight.shape[1]
    weighted_picks = own_picks * own_share[:, None, :]
    back_out = swap(partial_out.reshape(expert_devices, CAP, model_width).astype(BF)).astype(F32)
    back_in = swap(partial_in.reshape(expert_devices, CAP, model_width).astype(BF)).astype(F32)
    sum_out = back_out.reshape(EXP, group_size, CAP, model_width).sum(axis=1)
    sum_in = back_in.reshape(EXP, group_size, CAP, model_width).sum(axis=1)
    token_out = jnp.einsum("ect,ecd->td", weighted_picks, sum_out, precision=lax.Precision.HIGHEST)
    token_in = jnp.einsum("ect,ecd->td", own_picks, sum_in, precision=lax.Precision.HIGHEST)
    return (
        lax.psum_scatter(token_out.astype(BF), "section", scatter_dimension=1, tiled=True),
        lax.psum_scatter(token_in.astype(BF), "section", scatter_dimension=1, tiled=True),
        summed_grads[:, :hidden],
        summed_grads[:, hidden : 2 * hidden],
        summed_grads[:, 2 * hidden :],
    )


def pointwise(gate_pre, up_pre, act_grad):
    sigmoid_gate = jax.nn.sigmoid(gate_pre)
    silu_value = gate_pre * sigmoid_gate
    activation = (silu_value * up_pre).astype(BF)
    up_grad = (act_grad * silu_value).astype(BF)
    gate_grad = (act_grad * up_pre * sigmoid_gate * (1.0 + gate_pre * (1.0 - sigmoid_gate))).astype(BF)
    return activation, up_grad, gate_grad


def swap_expert(rows):
    size = lax.axis_size("expert")
    return lax.ppermute(rows, "expert", [(i, i ^ 1) for i in range(size)])


def swap_section(rows):
    return lax.ppermute(rows, "section", [(0, 1), (1, 0)])


def swap_plane(pieces):
    size = lax.axis_size("expert")
    both = [(s * size + i, (1 - s) * size + (i ^ 1)) for s in range(2) for i in range(size)]
    far = lax.ppermute(pieces[2], ("section", "expert"), both)
    return [swap_section(pieces[0]), swap_expert(pieces[1]), far]


ANYWHERE = pl.BlockSpec(memory_space=pl.ANY)
INSIDE = pl.BlockSpec(memory_space=pltpu.VMEM)


def params(mib):
    return pltpu.CompilerParams(vmem_limit_bytes=mib << 20)


def cost(flops, *arrays):
    moved = sum(a.size * a.dtype.itemsize for a in arrays)
    return pl.CostEstimate(flops=flops, bytes_accessed=moved, transcendentals=0)


def in_hbm(array):
    return pltpu.with_memory_space_constraint(array, pltpu.HBM)


def in_vmem(array):
    return pltpu.with_memory_space_constraint(array, pltpu.VMEM)


def pin_kernel(*refs):
    count = len(refs) // 2 - 1
    copies = [
        pltpu.make_async_copy(refs[i], refs[count + 1 + i], refs[-1].at[i]) for i in range(count)
    ]
    for copy in copies:
        copy.start()
    for copy in copies:
        copy.wait()


def pin(weights, after):
    count = len(weights)
    return pl.pallas_call(
        pin_kernel,
        out_shape=[pltpu.VMEM(weight.shape, weight.dtype) for weight in weights],
        in_specs=[ANYWHERE] * (count + 1),
        out_specs=[ANYWHERE] * count,
        scratch_shapes=[pltpu.SemaphoreType.DMA((count,))],
        cost_estimate=cost(0),
        compiler_params=params(1),
    )(*(in_hbm(weight) for weight in weights), after)


def gather_kernel(*refs):
    pieces, (w_ref, _, x_ref, out_ref) = refs[:-4][::-1], refs[-4:]
    rows = pieces[0].shape[0]
    for i, piece in enumerate(pieces):
        x_ref[i * rows : (i + 1) * rows] = piece[...]
    out_ref[...] = jnp.dot(x_ref[...], w_ref[...], preferred_element_type=F32).astype(BF)


def gather_project(pieces, weight, after):
    rows, (depth, hidden) = sum(piece.shape[0] for piece in pieces), weight.shape
    outs = [jax.ShapeDtypeStruct((rows, depth), BF), jax.ShapeDtypeStruct((rows, hidden), BF)]
    return pl.pallas_call(
        gather_kernel,
        out_shape=outs,
        in_specs=[INSIDE] * (len(pieces) + 1) + [ANYWHERE],
        out_specs=[INSIDE] * 2,
        cost_estimate=cost(0),
        compiler_params=params(14),
    )(*pieces[::-1], in_vmem(weight), after)


def project_kernel(x_ref, w_ref, out_ref):
    out_ref[...] = jnp.dot(x_ref[...], w_ref[...], preferred_element_type=F32).astype(BF)


def project(x, weight):
    rows, (depth, hidden) = x.shape[0], weight.shape
    out = jax.ShapeDtypeStruct((rows, hidden), BF)
    return pl.pallas_call(
        project_kernel,
        out_shape=out,
        in_specs=[INSIDE] * 2,
        out_specs=INSIDE,
        cost_estimate=cost(0),
        compiler_params=params(12),
    )(x, in_vmem(weight))


def iota(shape, dim):
    return lax.broadcasted_iota(jnp.int32, shape, dim)


def slot_rows(ids_ref, plane):
    count = ids_ref.shape[1]
    shape = (EXP * 2 * CAP, count)
    row = iota(shape, 0)
    place = row % (2 * CAP)
    expert = plane ^ (row // (2 * CAP))
    match = [ids_ref[j : j + 1, :] == expert for j in range(2)]
    chosen = jnp.logical_or(*match)
    before = (iota((count, count), 0) < iota((count, count), 1)).astype(F32)
    rank = jnp.dot(chosen.astype(F32), before, preferred_element_type=F32)
    picks = jnp.logical_and(chosen, rank == (place % CAP).astype(F32))
    return match, picks, place


def pack_kernel(*refs):
    hbm, out_refs, held, sem = refs[:4], refs[4 : 4 + EXP], refs[4 + EXP : 8 + EXP], refs[-1]
    half = out_refs[0].shape[1]
    cut = pl.ds(pl.multiple_of(lax.axis_index("section") * half, half), half)
    sources = [hbm[0].at[:, cut], hbm[1].at[:, cut], hbm[2], hbm[3]]
    copies = [pltpu.make_async_copy(a, b, sem.at[i]) for i, (a, b) in enumerate(zip(sources, held))]
    for copy in copies:
        copy.start()
    for copy in copies:
        copy.wait()
    tok_ref, grad_ref, ids_ref, probs_ref = held
    match, picks, place = slot_rows(ids_ref, lax.axis_index("expert") // 2)
    share = jnp.where(match[0], probs_ref[0:1, :], 0.0) + jnp.where(match[1], probs_ref[1:2, :], 0.0)
    scale = jnp.sum(jnp.where(picks, share, 0.0), axis=1, keepdims=True)
    picks = picks.astype(BF)
    tok = jnp.dot(picks, tok_ref[...], preferred_element_type=F32)
    grad = jnp.dot(picks, grad_ref[...], preferred_element_type=F32)
    payload = jnp.where(place[:, 0:1] < CAP, tok, grad * scale)
    for k, out_ref in enumerate(out_refs):
        out_ref[...] = payload[k * 2 * CAP : (k + 1) * 2 * CAP].astype(BF)


def pack(tokens, grad_out, expert_ids, gate_probs, half):
    outs = [jax.ShapeDtypeStruct((2 * CAP, half), BF)] * EXP
    rows = tokens.shape[0]
    given = (tokens, grad_out, expert_ids.T, gate_probs.T)
    return pl.pallas_call(
        pack_kernel,
        out_shape=outs,
        in_specs=[ANYWHERE] * 4,
        out_specs=[INSIDE] * EXP,
        scratch_shapes=[
            pltpu.VMEM((rows, half), BF),
            pltpu.VMEM((rows, half), BF),
            pltpu.VMEM((2, rows), jnp.int32),
            pltpu.VMEM((2, rows), F32),
            pltpu.SemaphoreType.DMA((4,)),
        ],
        cost_estimate=cost(0, tokens, grad_out, *outs),
        compiler_params=params(8),
    )(*(in_hbm(array) for array in given))


def sorting():
    n = EXP * CAP
    sorted_row, row = iota((2 * n, 2 * n), 0), iota((2 * n, 2 * n), 1)
    k, j = row // (2 * CAP), row % (2 * CAP)
    place = jnp.where(j < CAP, k * CAP + j, n + k * CAP + j - CAP)
    return (sorted_row == place).astype(BF)


def stack(refs, held_ref):
    rows = refs[0].shape[0]
    for i, ref in enumerate(refs):
        held_ref[i * rows : (i + 1) * rows] = ref[...].astype(F32)
    return held_ref[...].astype(BF)


def part_kernel(*refs):
    refs, (_, tok_ref, grad_ref, held_ref) = [refs[i] for i in (3, 2, 0, 1)], refs[EXP:]
    rows = jnp.dot(sorting(), stack(refs, held_ref), preferred_element_type=F32).astype(BF)
    n = EXP * CAP
    tok_ref[...] = rows[:n]
    grad_ref[...] = rows[n:]


def part(got, after):
    width = got[0].shape[1]
    outs = [jax.ShapeDtypeStruct((EXP * CAP, width), BF)] * 2
    return pl.pallas_call(
        part_kernel,
        out_shape=outs,
        in_specs=[INSIDE] * EXP + [ANYWHERE],
        out_specs=[INSIDE] * 2,
        scratch_shapes=[pltpu.VMEM((2 * EXP * CAP, width), F32)],
        cost_estimate=cost(0, *got, *outs),
        compiler_params=params(8),
    )(*[got[i] for i in (2, 3, 1, 0)], after)


def join_kernel(*refs):
    outs, ins, sent = refs[:4], refs[4:8], refs[8:]

    def total(pieces):
        return sum(p[...].astype(F32) for p in pieces).astype(BF)

    rows = jnp.concatenate([total(outs), total(ins)], axis=0)
    rows = lax.dot_general(
        sorting(), rows, (((0,), (0,)), ((), ())), preferred_element_type=F32
    )
    for k, ref in enumerate(sent):
        ref[...] = rows[k * 2 * CAP : (k + 1) * 2 * CAP].astype(BF)


def join(outs, ins):
    width = outs[0].shape[1]
    sent = [jax.ShapeDtypeStruct((2 * CAP, width), BF)] * EXP
    return pl.pallas_call(
        join_kernel,
        out_shape=sent,
        in_specs=[INSIDE] * 8,
        out_specs=[INSIDE] * EXP,
        cost_estimate=cost(0, *outs, *ins, *sent),
        compiler_params=params(10),
    )(*outs[::-1], *ins[::-1])


def unpack_kernel(*refs):
    refs, (ids_ref, probs_ref, out_ref, in_ref, held_ref) = refs[:EXP][::-1], refs[EXP:]
    match, picks, place = slot_rows(ids_ref, lax.axis_index("expert") // 2)
    rows = stack(refs, held_ref)
    count = ids_ref.shape[1]
    same = iota((count, count), 0) == iota((count, count), 1)
    probs = [
        jnp.sum(jnp.where(same, probs_ref[j : j + 1, :], 0.0), axis=1, keepdims=True)
        for j in range(2)
    ]

    first = place < CAP
    masks = [
        jnp.logical_and(picks, where).astype(BF)
        for where in (
            jnp.logical_and(first, match[0]),
            jnp.logical_and(first, match[1]),
            jnp.logical_not(first),
        )
    ]
    found = contract_rows(jnp.concatenate(masks, axis=1), rows)
    out_ref[...] = (probs[0] * found[:count] + probs[1] * found[count : 2 * count]).astype(BF)
    in_ref[...] = found[2 * count :].astype(BF)


def unpack(back, expert_ids, gate_probs):
    width = back[0].shape[1]
    outs = [jax.ShapeDtypeStruct((expert_ids.shape[0], width), BF)] * 2
    return pl.pallas_call(
        unpack_kernel,
        out_shape=outs,
        in_specs=[INSIDE] * (EXP + 2),
        out_specs=[INSIDE] * 2,
        scratch_shapes=[pltpu.VMEM((2 * EXP * CAP, width), F32)],
        cost_estimate=cost(0, *back, *outs),
        compiler_params=params(8),
    )(*back[::-1], expert_ids.T, gate_probs.T)


def spread(rows, refs):
    count = refs[0].shape[0]
    for i, ref in enumerate(refs):
        ref[...] = rows[i * count : (i + 1) * count].astype(BF)


def times_rows(lefts, weights, turned, refs):
    depth = weights[0].shape[0]
    tile = math.gcd(depth, TILE)
    for left, held in zip(lefts, turned):
        held[...] = left[...].T
    for at in range(0, depth, tile):
        cut = slice(at, at + tile)
        spread(
            sum(
                jnp.dot(weight[cut], held[...], preferred_element_type=F32)
                for weight, held in zip(weights, turned)
            )
            .astype(BF)
            .T,
            refs,
            cut,
        )


def spread(rows, refs, cut):
    count = refs[0].shape[0]
    for i, ref in enumerate(refs):
        ref[:, cut] = rows[i * count : (i + 1) * count]


def forward_kernel(g0_ref, g1_ref, u0_ref, u1_ref, w_ref, act_ref, silu_ref, slope_ref, *refs):
    hidden = act_ref.shape[1]
    tile = math.gcd(hidden, TILE)
    for at in range(0, hidden, tile):
        cut = slice(at, at + tile)
        gate_pre = g0_ref[:, cut].astype(F32) + g1_ref[:, cut].astype(F32)
        up_pre = u0_ref[:, cut].astype(F32) + u1_ref[:, cut].astype(F32)
        sigmoid_gate = jax.nn.sigmoid(gate_pre)
        silu_value = gate_pre * sigmoid_gate
        act_ref[:, cut] = (silu_value * up_pre).astype(BF)
        silu_ref[:, cut] = silu_value
        slope_ref[:, cut] = up_pre * sigmoid_gate * (1.0 + gate_pre * (1.0 - sigmoid_gate))
    times_rows([act_ref], [w_ref], refs[4:], refs[:4])


def forward(gates, ups, weight):
    rows, (depth, hidden) = gates[0].shape[0], weight.shape
    outs = [jax.ShapeDtypeStruct((rows, hidden), BF)]
    outs += [jax.ShapeDtypeStruct((rows, hidden), F32)] * 2
    outs += [jax.ShapeDtypeStruct((rows // 4, depth), BF)] * 4
    return pl.pallas_call(
        forward_kernel,
        out_shape=outs,
        in_specs=[INSIDE] * 5,
        out_specs=[INSIDE] * 7,
        scratch_shapes=[pltpu.VMEM((hidden, rows), BF)],
        cost_estimate=cost(0),
        compiler_params=params(18),
    )(*gates, *ups, in_vmem(weight))


def backward_kernel(
    a0_ref, a1_ref, silu_ref, slope_ref, wg_ref, wu_ref, dg_ref, du_ref, *refs
):
    hidden = dg_ref.shape[1]
    tile = math.gcd(hidden, TILE)
    for at in range(0, hidden, tile):
        cut = slice(at, at + tile)
        act_grad = a0_ref[:, cut].astype(F32) + a1_ref[:, cut].astype(F32)
        dg_ref[:, cut] = (act_grad * slope_ref[:, cut]).astype(BF)
        du_ref[:, cut] = (act_grad * silu_ref[:, cut]).astype(BF)
    times_rows([dg_ref, du_ref], [wg_ref, wu_ref], refs[4:], refs[:4])


def backward(acts, silu_value, slope, gate_weight, up_weight):
    rows, (depth, hidden) = acts[0].shape[0], gate_weight.shape
    outs = [jax.ShapeDtypeStruct((rows, hidden), BF)] * 2
    outs += [jax.ShapeDtypeStruct((rows // 4, depth), BF)] * 4
    return pl.pallas_call(
        backward_kernel,
        out_shape=outs,
        in_specs=[INSIDE] * 6,
        out_specs=[INSIDE] * 6,
        scratch_shapes=[pltpu.VMEM((hidden, rows), BF)] * 2,
        cost_estimate=cost(4 * rows * depth * hidden, *acts, silu_value, slope, *outs),
        compiler_params=params(20),
    )(*acts, silu_value, slope, in_vmem(gate_weight), in_vmem(up_weight))


def outer_kernel(*refs):
    count = (len(refs) - 4) // 2
    x_ref, y_refs, out_refs = refs[0], refs[1 : 1 + count], refs[1 + count : 1 + 2 * count]
    turned_ref, held_ref, sem = refs[-3:]
    depth = held_ref.shape[1]
    tile = math.gcd(depth, 256)
    turned_ref[...] = x_ref[...].T
    copies = []
    for j in range(count):
        for i, at in enumerate(range(0, depth, tile)):
            cut = slice(at, at + tile)
            held_ref[j, cut] = jnp.dot(
                turned_ref[cut], y_refs[j][...], preferred_element_type=F32
            ).astype(BF)
            copies.append(
                pltpu.make_async_copy(held_ref.at[j, cut], out_refs[j].at[cut], sem.at[j, i])
            )
            copies[-1].start()
    for copy in copies:
        copy.wait()


def outer(x, *ys):
    (rows, depth), hidden, count = x.shape, ys[0].shape[1], len(ys)
    outs = [jax.ShapeDtypeStruct((depth, hidden), BF)] * count
    return pl.pallas_call(
        outer_kernel,
        out_shape=outs,
        in_specs=[INSIDE] * (1 + count),
        out_specs=[ANYWHERE] * count,
        scratch_shapes=[
            pltpu.VMEM((depth, rows), BF),
            pltpu.VMEM((count, depth, hidden), BF),
            pltpu.SemaphoreType.DMA((count, depth // math.gcd(depth, 256))),
        ],
        cost_estimate=cost(2 * rows * depth * hidden * count, x, *ys, *outs),
        compiler_params=params(20 + 8 * count),
    )(x, *ys)


def swap_dp(rows):
    return lax.ppermute(rows, "dp", [(0, 1), (1, 0)])


def turn(pieces):
    size = lax.axis_size("expert")
    got = {}
    for k in reversed(range(EXP)):
        pairs = [
            ((s * size + i) * 2 + d, (d * size + (i ^ (2 * k))) * 2 + s)
            for s in range(2)
            for i in range(size)
            for d in range(2)
        ]
        got[k] = lax.ppermute(pieces[k], ("section", "expert", "dp"), pairs)
    return [got[k] for k in range(EXP)]


def paired(tokens, grad_out, expert_ids, gate_probs, gate_weight, up_weight, down_weight):
    payload = pack(tokens, grad_out, expert_ids, gate_probs, gate_weight.shape[0])
    got = turn(payload)
    own_t, own_g = part(got, payload[0])
    (gate_weight,) = pin((gate_weight,), own_t)

    slot_t, gate_part = gather_project([own_t] + swap_plane([own_t] * 3), gate_weight, own_t)
    gates = [gate_part, swap_dp(gate_part)]
    up_part = project(slot_t, up_weight)
    ups = [up_part, swap_dp(up_part)]
    activation, silu_value, slope, *part_out = forward(gates, ups, down_weight)
    slot_g, act_part = gather_project(
        [own_g] + swap_plane([own_g] * 3), down_weight, up_part
    )
    acts = [act_part, swap_dp(act_part)]
    part_out, _ = lax.optimization_barrier((part_out, act_part))
    gate_grad, up_grad, *part_in = backward(acts, silu_value, slope, gate_weight, up_weight)
    (grad_down,) = outer(slot_g, activation)
    grad_gate, grad_up = outer(slot_t, gate_grad, up_grad)
    sent = join(
        part_out[:1] + swap_plane(part_out[1:]), part_in[:1] + swap_plane(part_in[1:])
    )
    moe_out, grad_tokens = unpack(turn(sent), expert_ids, gate_probs)
    return moe_out, grad_tokens, grad_gate, grad_up, grad_down


def solution(mesh):
    sizes = mesh.shape
    pairs = sizes["section"] == 2 and sizes["dp"] == 2 and sizes["expert"] == 2 * EXP
    return jax.shard_map(
        paired if pairs else general,
        mesh=mesh,
        in_specs=(
            P(("expert", "dp"), None),
            P(("expert", "dp"), None),
            P(("expert", "dp"), None),
            P(("expert", "dp"), None),
            P("dp", ("expert", "section")),
            P("dp", ("expert", "section")),
            P("dp", ("expert", "section")),
        ),
        out_specs=(
            P(("expert", "dp"), "section"),
            P(("expert", "dp"), "section"),
            P("dp", ("expert", "section")),
            P("dp", ("expert", "section")),
            P("dp", ("expert", "section")),
        ),
        check_vma=False,
    )
```
